32 devices in a mesh: ctx: 16 (over z, y, x), fsdp: 2 (over core).
Axes of the slice: x: 2, y: 2, z: 4, core: 2. Of those that a mesh axis runs over, the one named last changes fastest.
Arguments:
- tokens_in: bfloat16 [6, 1024, 896], P('fsdp', 'ctx'), may hold values from -6 to 6
- cotangent: bfloat16 [6, 1024, 896], P('fsdp', 'ctx'), may hold values from -6 to 6
- block_order: int32 [32], replicated, may hold values from 0 to 31, as said below
- weight_query: float32 [896, 896], P(('ctx', 'fsdp')), may hold values from -0.25 to 0.25
- weight_key: float32 [896, 128], P(('ctx', 'fsdp')), may hold values from -0.25 to 0.25
- weight_value: float32 [896, 128], P(('ctx', 'fsdp')), may hold values from -0.1875 to 0.1875
- weight_out: float32 [896, 896], P(('ctx', 'fsdp')), may hold values from -1 to 1
- weight_gate: float32 [896, 4864], P(('ctx', 'fsdp')), may hold values from -0.1875 to 0.1875
- weight_up: float32 [896, 4864], P(('ctx', 'fsdp')), may hold values from -0.1875 to 0.1875
- weight_down: float32 [4864, 896], P(('ctx', 'fsdp')), may hold values from -0.078125 to 0.078125
- moment_query: float32 [896, 896], P(('ctx', 'fsdp')), may hold values from -24 to 24
- moment_key: float32 [896, 128], P(('ctx', 'fsdp')), may hold values from -1280 to 1280
- moment_value: float32 [896, 128], P(('ctx', 'fsdp')), may hold values from -1280 to 1280
- moment_out: float32 [896, 896], P(('ctx', 'fsdp')), may hold values from -112 to 112
- moment_gate: float32 [896, 4864], P(('ctx', 'fsdp')), may hold values from -96 to 96
- moment_up: float32 [896, 4864], P(('ctx', 'fsdp')), may hold values from -96 to 96
- moment_down: float32 [4864, 896], P(('ctx', 'fsdp')), may hold values from -224 to 224
- small_params: float32 [2944], P(('ctx', 'fsdp')), may hold values from -1.6 to 1.6, as said below
Outputs:
- activations: bfloat16 [6, 1024, 896], P('fsdp', 'ctx')
- input_grad: float32 [6, 1024, 896], P('fsdp', 'ctx')
- grad_query: float32 [896, 896], P(('ctx', 'fsdp'))
- grad_key: float32 [896, 128], P(('ctx', 'fsdp'))
- grad_value: float32 [896, 128], P(('ctx', 'fsdp'))
- grad_out: float32 [896, 896], P(('ctx', 'fsdp'))
- grad_gate: float32 [896, 4864], P(('ctx', 'fsdp'))
- grad_up: float32 [896, 4864], P(('ctx', 'fsdp'))
- grad_down: float32 [4864, 896], P(('ctx', 'fsdp'))
- new_query: float32 [896, 896], P(('ctx', 'fsdp'))
- new_key: float32 [896, 128], P(('ctx', 'fsdp'))
- new_value: float32 [896, 128], P(('ctx', 'fsdp'))
- new_out: float32 [896, 896], P(('ctx', 'fsdp'))
- new_gate: float32 [896, 4864], P(('ctx', 'fsdp'))
- new_up: float32 [896, 4864], P(('ctx', 'fsdp'))
- new_down: float32 [4864, 896], P(('ctx', 'fsdp'))
- new_mom_query: float32 [896, 896], P(('ctx', 'fsdp'))
- new_mom_key: float32 [896, 128], P(('ctx', 'fsdp'))
- new_mom_value: float32 [896, 128], P(('ctx', 'fsdp'))
- new_mom_out: float32 [896, 896], P(('ctx', 'fsdp'))
- new_mom_gate: float32 [896, 4864], P(('ctx', 'fsdp'))
- new_mom_up: float32 [896, 4864], P(('ctx', 'fsdp'))
- new_mom_down: float32 [4864, 896], P(('ctx', 'fsdp'))
- grad_small: float32 [2944], P(('ctx', 'fsdp'))
- new_small: float32 [2944], P(('ctx', 'fsdp'))
The draws below stay inside these ranges and needn't reach their ends.
Inputs may be any that keep to these rules, and one draw needn't show every extreme that they name: `block_order`: stored blocks 2 c and 2 c + 1 hold position blocks j and 31 - j for some j; every number appears once. `small_params`: the first 1792 entries are gains between 0.6 and 1.4.
All inputs are finite; a program needn't handle non-finite values.
Results may differ from the reference program's by a relative error of at most 0.017.
The reference program's roundings to bfloat16 on the way count: a program that leaves them out, or rounds other values in their place, can miss the bound.
Values may be sent and summed in bfloat16 or wider, within the bound.
No kernel may reach another device: no remote copies, remote signals or barrier semaphores. Data moves between devices by JAX's collectives and lax.ppermute only.
A program may use at most 256 MiB of HBM per device.

```python
import math
import jax
import jax.numpy as jnp
from jax import lax

D = 896
HEADS = 14
KV_HEADS = 2
HEAD_DIM = 64
FF = 4864
BLOCK = 32
NS_STEPS = 5
NSEQ = 6
BLOCKS = 32
SEQ_LEN = 1024
KVW = 128


def draw_block_order(key, part):
    key = jax.random.fold_in(key, 11)
    half_count = BLOCKS // 2
    shuffled = jax.random.permutation(key, half_count)
    paired = jnp.stack([shuffled, BLOCKS - 1 - shuffled], axis=1)
    return paired.reshape(BLOCKS).astype(jnp.int32)


def draw_small_params(key, part):
    key = jax.random.fold_in(key, 7)
    first_key, second_key = jax.random.split(key)
    gains = jnp.clip(1.0 + 0.15 * jax.random.normal(first_key, (2 * D,), jnp.float32), 0.6, 1.4)
    biases = jnp.clip(0.5 * jax.random.normal(second_key, (D + 2 * KVW,), jnp.float32), -1.6, 1.6)
    return jnp.concatenate([gains, biases]).astype(jnp.float32)


def shard_levels(key, shape, cuts, least, top_value):
    def one(dim, parts):
        heights = jax.random.uniform(jax.random.fold_in(jax.random.fold_in(key, 6), dim), (parts,), jnp.float32, least / len(cuts), top_value / len(cuts))
        return jnp.repeat(jnp.exp(heights), shape[dim] // parts).reshape((-1,) + (1,) * (len(shape) - dim - 1))

    factor_of = one(*cuts[0])
    for cut in cuts[1:]:
        factor_of = factor_of * one(*cut)
    return factor_of


def centred(rng, extent, width, reach, cuts=(), kind=jnp.bfloat16):
    entries = jax.random.normal(rng, extent, jnp.float32) * width
    if len(cuts) > 0:
        entries = shard_levels(rng, extent, cuts, -0.22, 0.18) * entries
    return jnp.clip(entries, min=-reach, max=reach).astype(kind)


def setup_inputs(seed: int = 0) -> dict:
    arg_keys = jax.random.split(jax.random.key(seed), 19)
    return {
        "tokens_in": centred(arg_keys[0], (NSEQ, SEQ_LEN, D), 1.0, 6.0, ((0, 2), (1, 16))),
        "cotangent": centred(arg_keys[1], (NSEQ, SEQ_LEN, D), 1.0, 6.0, ((0, 2), (1, 16))),
        "block_order": draw_block_order(jax.random.fold_in(arg_keys[18], 71), 0),
        "weight_query": centred(arg_keys[3], (D, D), (D // 2) ** -0.5, 0.25, ((0, 32),), jnp.float32),
        "weight_key": centred(arg_keys[4], (D, KVW), (D // 2) ** -0.5, 0.25, ((0, 32),), jnp.float32),
        "weight_value": centred(arg_keys[5], (D, KVW), D ** -0.5, 0.1875, ((0, 32),), jnp.float32),
        "weight_out": centred(arg_keys[6], (D, D), (D // 32) ** -0.5, 1.0, ((0, 32),), jnp.float32),
        "weight_gate": centred(arg_keys[7], (D, FF), D ** -0.5, 0.1875, ((0, 32),), jnp.float32),
        "weight_up": centred(arg_keys[8], (D, FF), D ** -0.5, 0.1875, ((0, 32),), jnp.float32),
        "weight_down": centred(arg_keys[9], (FF, D), FF ** -0.5, 0.078125, ((0, 32),), jnp.float32),
        "moment_query": centred(arg_keys[10], (D, D), ((NSEQ * SEQ_LEN) ** 0.5 / 20), 24.0, ((0, 32),), jnp.float32),
        "moment_key": centred(arg_keys[11], (D, KVW), (3 * (NSEQ * SEQ_LEN) ** 0.5), 1280.0, ((0, 32),), jnp.float32),
        "moment_value": centred(arg_keys[12], (D, KVW), (3 * (NSEQ * SEQ_LEN) ** 0.5), 1280.0, ((0, 32),), jnp.float32),
        "moment_out": centred(arg_keys[13], (D, D), ((NSEQ * SEQ_LEN) ** 0.5 / 4), 112.0, ((0, 32),), jnp.float32),
        "moment_gate": centred(arg_keys[14], (D, FF), ((NSEQ * SEQ_LEN) ** 0.5 / 5), 96.0, ((0, 32),), jnp.float32),
        "moment_up": centred(arg_keys[15], (D, FF), ((NSEQ * SEQ_LEN) ** 0.5 / 5), 96.0, ((0, 32),), jnp.float32),
        "moment_down": centred(arg_keys[16], (FF, D), ((NSEQ * SEQ_LEN) ** 0.5 / 2), 224.0, ((0, 32),), jnp.float32),
        "small_params": draw_small_params(jax.random.fold_in(arg_keys[18], 71), 0),
    }


@jax.custom_vjp
def low(v):
    return lax.optimization_barrier(v.astype(jnp.bfloat16)).astype(jnp.float32)

@jax.custom_vjp
def low_back(v):
    return v

def low_keep(v):
    return (low(v), None)

def low_pass(kept, grad):
    return (grad,)

def back_keep(v):
    return (v, None)

def back_low(kept, grad):
    return (low(grad),)
low.defvjp(low_keep, low_pass)
low_back.defvjp(back_keep, back_low)
highest_precision = lax.Precision.HIGHEST
theta_base = 1000000.0
norm_eps = 1e-06
ns_coeffs = (3.4445, -4.775, 2.0315)
momentum_decay = 0.95
muon_rate = 1.5
plain_rate = 2.0

def rope_tables(positions):
    frequency = theta_base ** (-jnp.arange(0, HEAD_DIM, 2, dtype=jnp.float32) / HEAD_DIM)
    angles = positions.astype(jnp.float32)[:, None] * frequency[None, :]
    angles = jnp.concatenate([angles, angles], axis=-1)
    return (jnp.cos(angles), jnp.sin(angles))

def rotate(values, cosine_table, sine_table):
    half_width = values.shape[-1] // 2
    turned = jnp.concatenate([-values[..., half_width:], values[..., :half_width]], axis=-1)
    return values * cosine_table + turned * sine_table

def attention(query_rot, key_rot, value_rows, positions):
    group_size = HEADS // KV_HEADS
    grouped = query_rot.reshape(SEQ_LEN, KV_HEADS, group_size, HEAD_DIM)
    query_span = math.gcd(SEQ_LEN, 512)
    query_blocks = grouped.reshape(SEQ_LEN // query_span, query_span, KV_HEADS, group_size, HEAD_DIM)
    pos_blocks = positions.reshape(SEQ_LEN // query_span, query_span)

    def one_block(block_args):
        query_block, query_pos = block_args
        scores = jnp.einsum('qhgd,khd->qhgk', query_block, key_rot, precision=highest_precision) * HEAD_DIM ** (-0.5)
        scores = low_back(scores)
        allowed = (positions[None, :] <= query_pos[:, None])[:, None, None, :]
        masked = jnp.where(allowed, scores, -jnp.inf)
        row_top = lax.optimization_barrier(jnp.max(masked, axis=-1, keepdims=True))
        expo_terms = jnp.exp(masked - row_top)
        probabilities = expo_terms / lax.optimization_barrier(jnp.sum(expo_terms, axis=-1, keepdims=True))
        return jnp.einsum('qhgk,khd->qhgd', low(probabilities), value_rows, precision=highest_precision)
    outcome = lax.map(jax.checkpoint(one_block), (query_blocks, pos_blocks))
    return outcome.reshape(SEQ_LEN, HEADS * HEAD_DIM)

def layer_sequence(sequence, low_weights, low_small, cos_table, sin_table, positions):
    query_mat, key_mat, value_mat, out_mat, gate_mat, up_mat, down_mat = low_weights
    gain_one = low_small[:D]
    gain_two = low_small[D:2 * D]
    bias_query = low_small[2 * D:3 * D]
    bias_key = low_small[3 * D:3 * D + KVW]
    bias_value = low_small[3 * D + KVW:]
    rescale_one = lax.rsqrt(lax.optimization_barrier(jnp.mean(sequence * sequence, axis=-1, keepdims=True)) + norm_eps)
    normed_one = low(sequence * rescale_one * gain_one)
    query_lin = low_back(jnp.dot(normed_one, query_mat, precision=highest_precision) + bias_query)
    key_lin = low_back(jnp.dot(normed_one, key_mat, precision=highest_precision) + bias_key)
    value_lin = low_back(jnp.dot(normed_one, value_mat, precision=highest_precision) + bias_value)
    cos_rows = cos_table[:, None, :]
    sin_rows = sin_table[:, None, :]
    query_rot = low(rotate(query_lin.reshape(SEQ_LEN, HEADS, HEAD_DIM), cos_rows, sin_rows))
    key_rot = low(rotate(key_lin.reshape(SEQ_LEN, KV_HEADS, HEAD_DIM), cos_rows, sin_rows))
    value_rows = low(value_lin).reshape(SEQ_LEN, KV_HEADS, HEAD_DIM)
    mixed = low(low_back(attention(query_rot, key_rot, value_rows, positions)))
    residual = sequence + low_back(jnp.dot(mixed, out_mat, precision=highest_precision))
    rescale_two = lax.rsqrt(lax.optimization_barrier(jnp.mean(residual * residual, axis=-1, keepdims=True)) + norm_eps)
    normed_two = low(residual * rescale_two * gain_two)
    gate_lin = low_back(jnp.dot(normed_two, gate_mat, precision=highest_precision))
    up_lin = low_back(jnp.dot(normed_two, up_mat, precision=highest_precision))
    hidden = low(gate_lin * lax.logistic(gate_lin) * up_lin)
    return residual + jnp.dot(hidden, down_mat, precision=highest_precision)

def orthogonalize(update):
    height, breadth = update.shape
    flipped = height > breadth
    matrix = update.T if flipped else update
    frobenius = jnp.sqrt(jnp.sum(matrix * matrix))
    current = matrix / (frobenius + 1e-07)
    alpha_term, beta_term, gamma_term = ns_coeffs
    for sweep_number in range(NS_STEPS):
        gram_matrix = jnp.dot(current, current.T, precision=highest_precision)
        square = jnp.dot(gram_matrix, gram_matrix, precision=highest_precision)
        polynomial = beta_term * gram_matrix + gamma_term * square
        current = alpha_term * current + jnp.dot(polynomial, current, precision=highest_precision)
    return current.T if flipped else current

def reference(tokens_in, cotangent, block_order, weight_query, weight_key, weight_value, weight_out, weight_gate, weight_up, weight_down, moment_query, moment_key, moment_value, moment_out, moment_gate, moment_up, moment_down, small_params):
    stored_index = jnp.arange(SEQ_LEN, dtype=jnp.int32)
    positions = block_order[stored_index // BLOCK] * BLOCK + stored_index % BLOCK
    cos_table, sin_table = rope_tables(positions)
    masters = (weight_query, weight_key, weight_value, weight_out, weight_gate, weight_up, weight_down)
    moments = (moment_query, moment_key, moment_value, moment_out, moment_gate, moment_up, moment_down)

    def forward(weights, small_vals, inputs):
        low_weights = tuple((low(weight) for weight in weights))
        low_small = low(small_vals)

        def one_sequence(sequence):
            return layer_sequence(sequence, low_weights, low_small, cos_table, sin_table, positions)
        return lax.map(jax.checkpoint(one_sequence), inputs)
    inputs = tokens_in.astype(jnp.float32)
    outcome, pullback = jax.vjp(forward, masters, small_params, inputs)
    gradients, grad_small, input_grad = pullback(cotangent.astype(jnp.float32))
    new_weights = []
    new_moments = []
    for weight, moment, gradient in zip(masters, moments, gradients):
        fresh_moment = momentum_decay * moment + gradient
        update = gradient + momentum_decay * fresh_moment
        orthogonal = orthogonalize(update)
        height, breadth = weight.shape
        factor = math.sqrt(max(1.0, breadth / height))
        new_weights.append(weight - muon_rate * (orthogonal * factor))
        new_moments.append(fresh_moment)
    new_small = small_params - plain_rate / math.sqrt(NSEQ * SEQ_LEN) * grad_small
    return (outcome.astype(jnp.bfloat16), input_grad, gradients[0], gradients[1], gradients[2], gradients[3], gradients[4], gradients[5], gradients[6], new_weights[0], new_weights[1], new_weights[2], new_weights[3], new_weights[4], new_weights[5], new_weights[6], new_moments[0], new_moments[1], new_moments[2], new_moments[3], new_moments[4], new_moments[5], new_moments[6], grad_small, new_small)
```

```python
import functools
import math

import jax
import jax.numpy as jnp
from jax import lax
from jax.experimental import pallas as pl
from jax.experimental.pallas import tpu as pltpu
from jax.sharding import Mesh
from jax.sharding import PartitionSpec as P

HEAD_DIM = 64
NS_STEPS = 5
LINE = 4
VMEM_LIMIT = 56 * 1024 * 1024

theta_base = 1000000.0
norm_eps = 1e-06
ns_coeffs = (3.4445, -4.775, 2.0315)
momentum_decay = 0.95
muon_rate = 1.5
plain_rate = 2.0

EVERY = ("r", "z", "xy", "f")
CTX = ("r", "z", "xy")
PLANE = ("xy", "f")
CHIPS = 4

f32 = jnp.float32
bf16 = jnp.bfloat16


def rope_tables(positions):
    frequency = theta_base ** (-jnp.arange(0, HEAD_DIM, 2, dtype=f32) / HEAD_DIM)
    angles = positions.astype(f32)[:, None] * frequency[None, :]
    return (jnp.cos(angles), jnp.sin(angles))


def dot_nn(left_side, right_side):
    return jnp.dot(left_side, right_side, preferred_element_type=f32)


def dot_tn(left_side, right_side):
    return lax.dot_general(
        left_side, right_side, (((0,), (0,)), ((), ())), preferred_element_type=f32
    )


def dot_nt(left_side, right_side):
    return lax.dot_general(
        left_side, right_side, (((1,), (1,)), ((), ())), preferred_element_type=f32
    )


def after(value, event):
    return lax.optimization_barrier((value, event))[0]


def exchange(parts, axes):
    return lax.all_to_all(parts, axes, split_axis=0, concat_axis=0, tiled=True)


def total(parts):
    return jnp.sum(parts.astype(f32), axis=0)


def swap(piece, axis, step, keep=None):
    count = lax.axis_size(axis)
    pairs = [(i, i ^ step) for i in range(count) if keep is None or keep(i, i ^ step)]
    return lax.ppermute(piece, axis, pairs)


def plane_swap(piece, step, depths):
    count = lax.axis_size("xy")
    pairs = [(z * count + i, z * count + (i ^ step)) for z in depths for i in range(count)]
    return lax.ppermute(piece, ("z", "xy"), pairs)


def gather_plane(piece):
    chips = [piece] + [swap(piece, "xy", step) for step in range(1, CHIPS)]
    return chips + [swap(each, "f", 1) for each in chips]


def place(parts, index):
    return lax.dynamic_index_in_dim(parts, index, 0, keepdims=False)


def gather_ctx(piece):
    if lax.axis_size("r") > 1:
        piece = lax.all_gather(piece, "r", axis=0, tiled=False)
    else:
        piece = piece[None]
    piece = jnp.concatenate([piece] + [swap(piece, "z", step) for step in range(1, LINE)], axis=0)
    return [piece] + [swap(piece, "xy", step) for step in range(1, CHIPS)]


def reduce_ctx(parts):
    repeat = lax.axis_size("r")
    chips = parts[0].astype(f32)
    for step in range(1, CHIPS):
        chips += swap(parts[step], "xy", step).astype(f32)
    chips = chips.reshape((LINE, repeat) + chips.shape[1:])
    low = chips.astype(bf16)
    own = chips[0]
    for step in range(1, LINE):
        own += swap(low[step], "z", step).astype(f32)
    if repeat > 1:
        own = lax.psum_scatter(own, "r", scatter_dimension=0, tiled=True)
    return own[0]


def plain_call(kernel, out_shape, scratch=(), **keywords):
    return pl.pallas_call(
        kernel,
        out_shape=out_shape,
        scratch_shapes=list(scratch),
        compiler_params=pltpu.CompilerParams(vmem_limit_bytes=VMEM_LIMIT),
        **keywords,
    )


def cost(flops, moved):
    return pl.CostEstimate(flops=int(flops), bytes_accessed=int(moved), transcendentals=0)


def like(shape, dtype):
    return jax.ShapeDtypeStruct(shape, dtype)


def turn(values):
    lane = lax.broadcasted_iota(jnp.int32, values.shape, 1)
    low_half = lane % HEAD_DIM < HEAD_DIM // 2
    right = pltpu.roll(values, HEAD_DIM // 2, 1)
    left = pltpu.roll(values, 2 * HEAD_DIM - HEAD_DIM // 2, 1)
    return jnp.where(low_half, left, right)


def normed(values):
    rescale = lax.rsqrt(jnp.mean(values * values, axis=1, keepdims=True) + norm_eps)
    return values * rescale, rescale


def norm_back(grad_normed, plain, rescale, gain):
    inner = grad_normed * gain
    grad_in = rescale * (inner - plain * jnp.mean(inner * plain, axis=1, keepdims=True))
    return grad_in, jnp.sum(grad_normed * plain, axis=0, keepdims=True)


def front_kernel(x_ref, w_ref, small_ref, cos_ref, sin_ref, q_ref, pair_ref, h_ref):
    seqs, heads, rows, _ = q_ref.shape
    width = x_ref.shape[1]
    wide = w_ref.shape[1] - width
    plain, _ = normed(x_ref[...].astype(f32))
    low = (plain * small_ref[:, :width]).astype(bf16)
    h_ref[...] = low
    lin = dot_nn(low, w_ref[:, :wide]) + small_ref[:, 2 * width :]
    pair = 2 * HEAD_DIM
    cosine, sine = cos_ref[...], sin_ref[...]
    for j in range(heads // 2 + 1):
        both = lin[:, j * pair : (j + 1) * pair]
        both = (both * cosine + turn(both) * sine).astype(bf16)
        for b in range(seqs):
            span = slice(b * rows, (b + 1) * rows)
            for k in range(2):
                head = both[span, k * HEAD_DIM : (k + 1) * HEAD_DIM]
                if j < heads // 2:
                    q_ref[b, 2 * j + k] = head
                else:
                    start = wide - pair + k * HEAD_DIM
                    value = lin[span, start : start + HEAD_DIM].astype(bf16)
                    pair_ref[b, k] = jnp.concatenate([head, value], axis=1)


def middle_kernel(o_ref, x_ref, w_ref, small_ref, low_ref, x1_ref, h_ref):
    seqs, heads, rows, _ = o_ref.shape
    width = x_ref.shape[1]
    pair = 2 * HEAD_DIM
    for b in range(seqs):
        for j in range(heads // 2):
            both = jnp.concatenate([o_ref[b, 2 * j], o_ref[b, 2 * j + 1]], axis=1)
            low_ref[b * rows : (b + 1) * rows, j * pair : (j + 1) * pair] = both
    wide = w_ref.shape[1] - width
    residual = x_ref[...].astype(f32) + dot_nn(low_ref[...], w_ref[:, wide:])
    x1_ref[...] = residual
    plain, _ = normed(residual)
    h_ref[...] = (plain * small_ref[:, width : 2 * width]).astype(bf16)


def fold_kernel(a_ref, b_ref, own_ref, *low_refs):
    rows = own_ref.shape[0]
    own_ref[...] = a_ref[:rows].astype(f32) + b_ref[:rows].astype(f32)
    for step, ref in enumerate(low_refs, 1):
        span = slice(step * rows, (step + 1) * rows)
        ref[...] = (a_ref[span].astype(f32) + b_ref[span].astype(f32)).astype(bf16)


def fold(first, second):
    rows, width = first.shape
    rows //= CHIPS
    return plain_call(
        fold_kernel, [like((rows, width), f32)] + [like((rows, width), bf16)] * (CHIPS - 1)
    )(first, second)


def join_kernel(qa_ref, qb_ref, ka_ref, kb_ref, own_ref, *low_refs):
    rows, wide = qa_ref.shape[2:]
    for step, ref in enumerate((own_ref,) + low_refs):
        query = qa_ref[step].astype(f32) + qb_ref[step].astype(f32)
        other = ka_ref[step].astype(f32) + kb_ref[step].astype(f32)
        ref[:, :rows, :wide] = query.astype(ref.dtype)
        ref[:, rows:, :wide] = jnp.zeros(ref[:, rows:, :wide].shape, ref.dtype)
        ref[:, :, wide:] = other.astype(ref.dtype)


def join(query_first, query_second, other_first, other_second):
    depth, rows, wide = query_first.shape[1:]
    shape = (depth, rows + 1, wide + other_first.shape[3])
    return plain_call(join_kernel, [like(shape, f32)] + [like(shape, bf16)] * (CHIPS - 1))(
        query_first, query_second, other_first, other_second
    )


def spread_kernel(own_ref, a_ref, b_ref, c_ref, out_ref, *low_refs):
    repeat = out_ref.shape[0]
    for step, ref in enumerate((out_ref,) + low_refs):
        for r in range(repeat):
            q = r * LINE + step
            value = own_ref[q] + a_ref[q].astype(f32) + b_ref[q].astype(f32) + c_ref[q].astype(f32)
            ref[r] = value.astype(ref.dtype)


def spread(own, arrived, repeat):
    shape = (repeat,) + own.shape[1:]
    return plain_call(spread_kernel, [like(shape, f32)] + [like(shape, bf16)] * (LINE - 1))(
        own, *arrived
    )


def step_kernel(core_ref, own_ref, a_ref, b_ref, c_ref, *refs):
    moments, grads, fresh_refs = refs[:4], refs[4:8], refs[8:12]
    small_ref, mine_ref, other_ref = refs[12:]
    rows = moments[0].shape[0]
    total_sum = own_ref[0] + a_ref[0].astype(f32) + b_ref[0].astype(f32) + c_ref[0].astype(f32)
    width = moments[0].shape[1]
    narrow = moments[1].shape[1]
    starts = (0, 2 * width, 2 * width + narrow, width)
    small_ref[...] = total_sum[rows:, 2 * width :]
    updates = []
    for m_ref, g_ref, n_ref, start in zip(moments, grads, fresh_refs, starts):
        grad = total_sum[:rows, start : start + m_ref.shape[1]]
        fresh = momentum_decay * m_ref[...] + grad
        g_ref[...] = grad
        n_ref[...] = fresh
        updates.append((grad + momentum_decay * fresh).astype(bf16))
    query, key, value, out = updates
    first = jnp.concatenate([query, key], axis=1)
    second = jnp.concatenate([out, value], axis=1)

    @pl.when(core_ref[0] == 0)
    def _():
        mine_ref[...] = first
        other_ref[...] = second

    @pl.when(core_ref[0] != 0)
    def _():
        mine_ref[...] = second
        other_ref[...] = first


def step_of(core, own, arrived, moments):
    rows = moments[0].shape[0]
    shapes = [like(m.shape, f32) for m in moments]
    pair_width = moments[0].shape[1] + moments[1].shape[1]
    vmem = pl.BlockSpec(memory_space=pltpu.VMEM)
    outs = plain_call(
        step_kernel,
        shapes
        + shapes
        + [like((1, 2 * moments[1].shape[1]), f32)]
        + [like((rows, pair_width), bf16)] * 2,
        in_specs=[pl.BlockSpec(memory_space=pltpu.SMEM)] + [vmem] * 8,
    )(core, own, *arrived, *moments)
    return outs[:4], outs[4:8], outs[8], outs[9], outs[10]


def turnback_kernel(
    own_ref, a_ref, b_ref, c_ref, x1_ref, dy_ref, w_ref, small_ref, dx_ref, da_ref, do_ref, gain_ref
):
    seqs, heads, rows, _ = do_ref.shape
    width = x1_ref.shape[1]
    wide = w_ref.shape[1] - width
    grad = own_ref[...] + a_ref[...].astype(f32) + b_ref[...].astype(f32) + c_ref[...].astype(f32)
    plain, rescale = normed(x1_ref[...])
    grad_in, grad_gain = norm_back(grad, plain, rescale, small_ref[:, width : 2 * width])
    gain_ref[...] = grad_gain
    grad_residual = dy_ref[...].astype(f32) + grad_in
    dx_ref[...] = grad_residual
    low = grad_residual.astype(bf16)
    da_ref[...] = low
    mixed = dot_nt(low, w_ref[:, wide:]).astype(bf16)
    for b in range(seqs):
        for j in range(heads):
            start = j * HEAD_DIM
            do_ref[b, j] = mixed[b * rows : (b + 1) * rows, start : start + HEAD_DIM]


def shard_rows(here_ref, refs, value, rows, column, first):
    chips, depth = refs[0].shape[:2]
    cores = len(refs)
    core, chip, line = here_ref[0], here_ref[1], here_ref[2]
    for k in range(cores):
        for target, ref in enumerate(refs):

            @pl.when((core ^ k) == target)
            def _():
                for q in range(depth):
                    for c in range(chips):
                        start = ((q * chips + c) * cores + k) * rows
                        at = (q // LINE) * LINE + ((q % LINE) ^ line)
                        piece = value[start : start + rows] if first else value(start // rows)
                        span = slice(0, rows) if first else slice(ref.shape[2] - 1, ref.shape[2])
                        ref[c ^ chip, at, span, column : column + piece.shape[1]] = piece


def query_kernel(
    here_ref, h_ref, dq_ref, o_ref, da_ref, cos_ref, sin_ref, lin_ref, own_ref, other_ref
):
    seqs, heads, rows, _ = dq_ref.shape
    width = h_ref.shape[1]
    pair = 2 * HEAD_DIM
    for b in range(seqs):
        span = slice(b * rows, (b + 1) * rows)
        cosine, sine = cos_ref[span], sin_ref[span]
        for j in range(heads // 2):
            both = jnp.concatenate([dq_ref[b, 2 * j], dq_ref[b, 2 * j + 1]], axis=1)
            both = both * cosine - turn(both) * sine
            lin_ref[span, j * pair : (j + 1) * pair] = both.astype(bf16)
    rows = own_ref.shape[2]
    query = dot_tn(h_ref[...], lin_ref[...]).astype(bf16)
    shard_rows(here_ref, (own_ref, other_ref), query, rows, 0, True)
    out = dot_tn(o_ref[...], da_ref[...]).astype(bf16)
    shard_rows(here_ref, (own_ref, other_ref), out, rows, width, True)


def back_kernel(
    here_ref,
    pair_ref,
    lin_ref,
    h_ref,
    x_ref,
    dx_ref,
    w_ref,
    small_ref,
    cos_ref,
    sin_ref,
    gain_ref,
    out_ref,
    own_ref,
    other_ref,
    all_lin,
    all_small,
):
    seqs, kv_heads, rows, pair = pair_ref.shape
    width = x_ref.shape[1]
    wide = w_ref.shape[1] - width
    all_lin[:, :width] = lin_ref[...]
    for b in range(seqs):
        span = slice(b * rows, (b + 1) * rows)
        first, second = pair_ref[b, 0], pair_ref[b, 1]
        keys = jnp.concatenate([first[:, :HEAD_DIM], second[:, :HEAD_DIM]], axis=1)
        values = jnp.concatenate([first[:, HEAD_DIM:], second[:, HEAD_DIM:]], axis=1)
        keys = keys * cos_ref[span] - turn(keys) * sin_ref[span]
        all_lin[span, width : width + pair] = keys.astype(bf16)
        all_lin[span, width + pair :] = values.astype(bf16)
    lin = all_lin[...]
    grad = dot_nt(lin, w_ref[:, :wide])
    plain, rescale = normed(x_ref[...].astype(f32))
    grad_in, grad_gain = norm_back(grad, plain, rescale, small_ref[:, :width])
    out_ref[...] = dx_ref[...] + grad_in
    all_small[:, :width] = grad_gain
    all_small[:, width : 2 * width] = gain_ref[...]
    all_small[:, 2 * width :] = jnp.sum(lin.astype(f32), axis=0, keepdims=True)
    refs = (own_ref, other_ref)
    chips, depth, rows, _ = own_ref.shape
    for ref in refs:
        ref[...] = jnp.zeros_like(ref)
    grads = dot_tn(h_ref[...], lin[:, width:]).astype(bf16)
    shard_rows(here_ref, refs, grads, rows - 1, 0, True)
    small_rows = all_small.shape[1] // (2 * chips * depth)

    def small_of(number):
        return all_small[:, number * small_rows : (number + 1) * small_rows].astype(bf16)

    shard_rows(here_ref, refs, small_of, 1, 0, False)


def softmax_keys(keys, queries, key_pos, query_pos):
    scores = dot_nt(keys, queries) * (HEAD_DIM ** (-0.5))
    masked = jnp.where(key_pos <= query_pos, scores, -1e30)
    terms = jnp.exp(masked - jnp.max(masked, axis=0, keepdims=True))
    return terms * (1.0 / jnp.sum(terms, axis=0, keepdims=True))


def joined_pairs(refs):
    return jnp.concatenate([ref[...].reshape(-1, ref.shape[-1]) for ref in refs], axis=0)


def attend_kernel(q_ref, *refs):
    kv_refs, (kpos_ref, qpos_ref, o_ref) = refs[:CHIPS], refs[CHIPS:]
    group, rows, width = q_ref.shape[1:]
    queries = q_ref[...].reshape(group * rows, width)
    pairs = joined_pairs(kv_refs)
    probs = softmax_keys(pairs[:, :width], queries, kpos_ref[...], qpos_ref[...]).astype(bf16)
    mixed = dot_nn(pairs.T[width:], probs)
    o_ref[...] = mixed.T.reshape(1, group, rows, width).astype(bf16)


def attend_back_kernel(q_ref, do_ref, *refs):
    kv_refs, (kpos_ref, qpos_ref, dq_ref), dkv_refs = (
        refs[:CHIPS],
        refs[CHIPS : CHIPS + 3],
        refs[CHIPS + 3 :],
    )
    group, rows, width = q_ref.shape[1:]
    queries = q_ref[...].reshape(group * rows, width)
    grads = do_ref[...].reshape(group * rows, width)
    pairs = joined_pairs(kv_refs)
    probs = softmax_keys(pairs[:, :width], queries, kpos_ref[...], qpos_ref[...])
    grad_probs = dot_nt(pairs[:, width:], grads)
    delta = jnp.sum(probs * grad_probs, axis=0, keepdims=True)
    grad_scores = (probs * (grad_probs - delta)).astype(bf16)
    scale = HEAD_DIM ** (-0.5)
    grad_keys = dot_nn(grad_scores, queries) * scale
    grad_values = dot_nn(probs.astype(bf16), grads)
    both = jnp.concatenate([grad_keys, grad_values], axis=1).astype(bf16)
    span = both.shape[0] // CHIPS
    for number, ref in enumerate(dkv_refs):
        ref[...] = both[number * span : (number + 1) * span].reshape(ref.shape)
    grad_queries = dot_nn(pairs.T[:width], grad_scores) * scale
    dq_ref[...] = grad_queries.T.reshape(dq_ref.shape)


def attention_specs(queries, pairs):
    _, heads, rows, _ = queries.shape
    chunks, _, kv_heads = pairs.shape[:3]
    group = heads // kv_heads
    length = CHIPS * chunks * rows
    q_spec = pl.BlockSpec((1, group, rows, HEAD_DIM), lambda b, h: (b, h, 0, 0))
    kv_spec = pl.BlockSpec((chunks, 1, 1, rows, 2 * HEAD_DIM), lambda b, h: (0, b, h, 0, 0))
    kpos_spec = pl.BlockSpec((length, 1), lambda b, h: (0, 0))
    qpos_spec = pl.BlockSpec((1, group * rows), lambda b, h: (0, 0))
    return q_spec, kv_spec, kpos_spec, qpos_spec


def attend(queries, pairs, key_pos, query_pos):
    q_spec, kv_spec, kpos_spec, qpos_spec = attention_specs(queries, pairs[0])
    scores = queries.shape[0] * queries.shape[1] * queries.shape[2] * key_pos.shape[0]
    return plain_call(
        attend_kernel,
        like(queries.shape, bf16),
        grid=(queries.shape[0], pairs[0].shape[2]),
        in_specs=[q_spec] + [kv_spec] * CHIPS + [kpos_spec, qpos_spec],
        out_specs=q_spec,
        cost_estimate=cost(scores * 16 * HEAD_DIM, scores * 8),
    )(queries, *pairs, key_pos, query_pos)


def attend_back(queries, grads, pairs, key_pos, query_pos):
    q_spec, kv_spec, kpos_spec, qpos_spec = attention_specs(queries, pairs[0])
    scores = queries.shape[0] * queries.shape[1] * queries.shape[2] * key_pos.shape[0]
    outs = plain_call(
        attend_back_kernel,
        [like(queries.shape, f32)] + [like(pairs[0].shape, bf16)] * CHIPS,
        grid=(queries.shape[0], pairs[0].shape[2]),
        in_specs=[q_spec, q_spec] + [kv_spec] * CHIPS + [kpos_spec, qpos_spec],
        out_specs=[q_spec] + [kv_spec] * CHIPS,
        cost_estimate=cost(scores * 40 * HEAD_DIM, scores * 12),
    )(queries, grads, *pairs, key_pos, query_pos)
    return outs[0], outs[1:]


def feed_kernel(count, *refs):
    h_refs, (order_ref, dy_ref, wgu_ref, wd_ref) = refs[:count], refs[count : count + 4]
    y_refs = refs[count + 4 : count + 6]
    dh_refs = refs[count + 6 : count + 8]
    gg_ref, gu_ref, gd_ref, agu, ad, h_all, dy_all, sems = refs[count + 8 :]
    step = pl.program_id(0)
    rows = h_refs[0].shape[0]
    tile = y_refs[0].shape[0]
    each = tile // rows

    def copies(number):
        span = pl.ds(number * rows, rows)
        return (
            pltpu.make_async_copy(h_refs[number], h_all.at[span], sems.at[0, number]),
            pltpu.make_async_copy(dy_ref.at[order_ref[number]], dy_all.at[span], sems.at[1, number]),
        )

    @pl.when(step == 0)
    def _():
        for number in range(count):
            for copy in copies(number):
                copy.start()
        agu[...] = jnp.zeros_like(agu)
        ad[...] = jnp.zeros_like(ad)

    for number in range(count):

        @pl.when(step == number // each)
        def _():
            for copy in copies(number):
                copy.wait()

    start = pl.multiple_of(step * tile, tile)
    normed_rows = h_all[pl.ds(start, tile)]
    grads = dy_all[pl.ds(start, tile)]
    units = wgu_ref.shape[3]
    gate_mat = wgu_ref[:, 0].reshape(-1, units)
    up_mat = wgu_ref[:, 1].reshape(-1, units)
    gate = dot_nn(normed_rows, gate_mat)
    up = dot_nn(normed_rows, up_mat)
    sigmoid = 1.0 / (1.0 + jnp.exp(-gate))
    silu = gate * sigmoid
    hidden = (silu * up).astype(bf16)
    grad_hidden = dot_nt(grads, wd_ref[...])
    grad_gate = (grad_hidden * up * sigmoid * (1.0 + gate * (1.0 - sigmoid))).astype(bf16)
    grad_up = (grad_hidden * silu).astype(bf16)
    dh = (dot_nt(grad_gate, gate_mat) + dot_nt(grad_up, up_mat)).astype(bf16)
    y = dot_nn(hidden, wd_ref[...]).astype(bf16)
    for core in range(2):

        @pl.when(step // (pl.num_programs(0) // 2) == core)
        def _():
            y_refs[core][...] = y
            dh_refs[core][...] = dh

    agu[0] += dot_tn(normed_rows, grad_gate)
    agu[1] += dot_tn(normed_rows, grad_up)
    ad[...] += dot_tn(hidden, grads)

    @pl.when(step == pl.num_programs(0) - 1)
    def _():
        gg_ref[...] = agu[0].astype(bf16)
        gu_ref[...] = agu[1].astype(bf16)
        gd_ref[...] = ad[...].astype(bf16)


def feed_forward(normed_rows, order, grads, gate_up, down_mat):
    count = len(normed_rows)
    rows, width = normed_rows[0].shape
    units = gate_up.shape[3]
    tokens = count * rows
    tile = CHIPS * rows
    steps = count // CHIPS
    half = tokens // 2
    first = pl.BlockSpec((tile, width), lambda t: (jnp.minimum(t, steps // 2 - 1), 0))
    second = pl.BlockSpec((tile, width), lambda t: (jnp.maximum(t - steps // 2, 0), 0))
    weights = pl.BlockSpec(gate_up.shape, lambda t: (0, 0, 0, 0))
    wide = pl.BlockSpec((width, units), lambda t: (0, 0))
    tall = pl.BlockSpec((units, width), lambda t: (0, 0))
    anywhere = pl.BlockSpec(memory_space=pl.ANY)
    outs = plain_call(
        functools.partial(feed_kernel, count),
        [like((half, width), bf16)] * 4
        + [like((width, units), bf16)] * 2
        + [like((units, width), bf16)],
        [
            pltpu.VMEM((2, width, units), f32),
            pltpu.VMEM((units, width), f32),
            pltpu.VMEM((tokens, width), bf16),
            pltpu.VMEM((tokens, width), bf16),
            pltpu.SemaphoreType.DMA((2, count)),
        ],
        grid=(steps,),
        in_specs=[anywhere] * count
        + [pl.BlockSpec(memory_space=pltpu.SMEM), anywhere, weights, tall],
        out_specs=[first, second, first, second, wide, wide, tall],
        cost_estimate=cost(36 * tokens * width * units, 8 * tokens * width + 12 * units * width),
    )(*normed_rows, order, grads, gate_up, down_mat)
    return outs[:2], outs[2:4], outs[4:]


def update_kernel(span, in_ref, mg_ref, mu_ref, gg_ref, gu_ref, ng_ref, nu_ref, u_ref):
    plane, _, _, units = in_ref.shape
    depth = units // span
    triples = ((mg_ref, gg_ref, ng_ref), (mu_ref, gu_ref, nu_ref))
    for which, (m_ref, g_ref, n_ref) in enumerate(triples):
        for q in range(depth):
            for p in range(plane):
                start = (q * plane + p) * span
                piece = in_ref[p, which, :, q * span : (q + 1) * span]
                g_ref[:, start : start + span] = piece.astype(f32)
        grad = g_ref[...]
        fresh = momentum_decay * m_ref[...] + grad
        n_ref[...] = fresh
        u_ref[which] = (grad + momentum_decay * fresh).astype(bf16)


def wide_update(arrived, moment_gate, moment_up, span):
    rows, columns = moment_gate.shape
    return plain_call(
        functools.partial(update_kernel, span),
        [like((rows, columns), f32)] * 4 + [like((2, rows, columns), bf16)],
    )(arrived, moment_gate, moment_up)


def row_spans(size):
    first = size % 256
    bounds = ([0, first] if first else [0]) + list(range(first + 256, size + 1, 256))
    return list(zip(bounds[:-1], bounds[1:]))


def poly_scratch(count, size):
    return [pltpu.VMEM((count, size, size), bf16)] * 6 + [pltpu.VMEM((2, count, size, size), bf16)] * 2


def poly_core(count, size, load, write, scratch):
    a_hi, a_lo, p_hi, p_lo, t_hi, t_lo, q_hi, q_lo = scratch
    alpha_term, beta_term, gamma_term = ns_coeffs
    spans = row_spans(size)

    def eye_of(start, stop):
        row = lax.broadcasted_iota(jnp.int32, (stop - start, size - start), 0)
        col = lax.broadcasted_iota(jnp.int32, (stop - start, size - start), 1)
        return row == col

    def store(high, low, i, start, stop, value):
        rounded = value.astype(bf16)
        rest = (value - rounded.astype(f32)).astype(bf16)
        high[i, start:stop, start:] = rounded
        low[i, start:stop, start:] = rest
        if stop < size:
            turned = value[:, stop - start :].T
            rounded = turned.astype(bf16)
            high[i, stop:, start:stop] = rounded
            low[i, stop:, start:stop] = (turned - rounded.astype(f32)).astype(bf16)

    def product(left, right, i, start, stop):
        left_hi, left_lo = left[0][i, start:stop, :], left[1][i, start:stop, :]
        right_hi, right_lo = right[0][i, :, start:], right[1][i, :, start:]
        return (
            dot_nn(left_hi, right_lo) + dot_nn(left_lo, right_hi) + dot_nn(left_hi, right_hi)
        )

    grams = (a_hi, a_lo)
    poly = (p_hi, p_lo)
    once = (t_hi, t_lo)
    inverses = []
    for i in range(count):
        squares = jnp.zeros((1, 1), f32)
        for start, stop in spans:
            diagonal = jnp.where(eye_of(start, stop), load(i, start, stop), 0.0)
            squares += jnp.sum(jnp.sum(diagonal, axis=1, keepdims=True), axis=0, keepdims=True)
        inverse = 1.0 / (jnp.sqrt(squares) + 1e-07)
        inverses.append(inverse)
        for start, stop in spans:
            store(*grams, i, start, stop, load(i, start, stop) * (inverse * inverse))

    for sweep in range(NS_STEPS):
        now, later = sweep % 2, (sweep + 1) % 2
        old = (q_hi.at[later], q_lo.at[later])
        new = (q_hi.at[now], q_lo.at[now])
        for start, stop in spans:
            for i in range(count):
                value = gamma_term * product(grams, grams, i, start, stop)
                mine = a_hi[i, start:stop, start:].astype(f32)
                mine += a_lo[i, start:stop, start:].astype(f32)
                value += beta_term * mine
                value += jnp.where(eye_of(start, stop), alpha_term, 0.0)
                store(*poly, i, start, stop, value)
                if sweep == 0:
                    store(*new, i, start, stop, value * inverses[i])
        last = sweep == NS_STEPS - 1
        if sweep > 0:
            for start, stop in spans:
                for i in range(count):
                    value = product(old, poly, i, start, stop)
                    if not last:
                        store(*new, i, start, stop, value)
                    else:
                        write(i, slice(start, stop), slice(start, size), value)
                        if stop < size:
                            turned = value[:, stop - start :].T
                            write(i, slice(stop, size), slice(start, stop), turned)
        if not last:
            for left, target in ((grams, once), (once, grams)):
                for start, stop in spans:
                    for i in range(count):
                        store(*target, i, start, stop, product(left, poly, i, start, stop))


def load_blocks(refs, target, sem):
    rows = refs[0].shape[0]
    return [
        pltpu.make_async_copy(ref, target.at[pl.ds(number * rows, rows)], sem.at[number])
        for number, ref in enumerate(refs)
    ]


def gram_kernel(mode_ref, *refs):
    groups = [refs[:CHIPS], refs[CHIPS : 2 * CHIPS], refs[2 * CHIPS : 3 * CHIPS]]
    out_ref, narrow_ref, *scratch, sem = refs[3 * CHIPS :]
    spans = row_spans(out_ref.shape[0])
    for number, (group, whole) in enumerate(zip(groups, scratch)):

        @pl.when(mode_ref[0] == number)
        def _():
            copies = load_blocks(group, whole, sem)
            for copy in copies:
                copy.start()
            for copy in copies:
                copy.wait()
            for start, stop in spans:
                if number == 1:
                    block = dot_tn(whole[:, start:stop], whole[:, start:])
                elif number == 0:
                    block = dot_nt(whole[start:stop], whole[start:])
                else:
                    size = out_ref.shape[0]
                    block = dot_nt(whole[start:stop, :size], whole[start:, :size])
                out_ref[start:stop, start:] = block
            if number == 2:
                narrow = whole[:, out_ref.shape[0] :]
                narrow_ref[...] = dot_tn(narrow, narrow)


def gram_of(mode, wide, tall, square):
    size = tall[0].shape[1]
    narrow = square[0].shape[1] - size
    spec = [pl.BlockSpec(memory_space=pltpu.SMEM)]
    spec += [pl.BlockSpec(memory_space=pl.ANY)] * (3 * CHIPS)
    groups = (wide, tall, square)
    scratch = [
        pltpu.VMEM((CHIPS * group[0].shape[0], group[0].shape[1]), bf16) for group in groups
    ]
    return plain_call(
        gram_kernel,
        [like((size, size), f32), like((narrow, narrow), f32)],
        scratch + [pltpu.SemaphoreType.DMA((CHIPS,))],
        in_specs=spec,
        cost_estimate=cost(4 * size * size * size * 3, 8 * size * size),
    )(mode, *wide, *tall, *square)


def ortho_kernel(mode_ref, a_ref, b_ref, n_ref, *refs):
    wide, tall, square = refs[:CHIPS], refs[CHIPS : CHIPS + 1], refs[CHIPS + 1 : 2 * CHIPS + 1]
    outs = refs[2 * CHIPS + 1 : 2 * CHIPS + 4]
    q_ref, k_ref, *wholes, sem = refs[2 * CHIPS + 4 : 2 * CHIPS + 10]
    scratch = refs[2 * CHIPS + 10 : 2 * CHIPS + 18]
    narrow_scratch = refs[2 * CHIPS + 18 :]
    groups = (wide, tall, square)
    for number, (group, whole) in enumerate(zip(groups, wholes)):

        @pl.when(mode_ref[0] == number)
        def _():
            for copy in load_blocks(group, whole, sem):
                copy.start()

    def load(i, start, stop):
        return a_ref[start:stop, start:] + b_ref[start:stop, start:]

    def write(i, rows, columns, value):
        q_ref[rows, columns] = value.astype(bf16)

    size = a_ref.shape[0]
    poly_core(1, size, load, write, scratch)

    @pl.when(mode_ref[0] == 2)
    def _():
        def narrow_load(i, start, stop):
            return n_ref[start:stop, start:]

        def narrow_write(i, rows, columns, value):
            k_ref[rows, columns] = value.astype(bf16)

        poly_core(1, n_ref.shape[0], narrow_load, narrow_write, narrow_scratch)

    for number, (group, whole, out_ref) in enumerate(zip(groups, wholes, outs)):

        @pl.when(mode_ref[0] == number)
        def _():
            for copy in load_blocks(group, whole, sem):
                copy.wait()
            if number == 1:
                out_ref[...] = dot_nn(whole[...], q_ref[...]).astype(bf16)
            elif number == 0:
                rows = q_ref[: out_ref.shape[0], :]
                out_ref[...] = dot_nn(rows, whole[...]).astype(bf16)
            else:
                count = out_ref.shape[0]
                rows = q_ref[:count, :]
                out_ref[:, :size] = dot_nn(rows, whole[:, :size]).astype(bf16)
                out_ref[:, size:] = dot_nn(whole[:count, size:], k_ref[...]).astype(bf16)


def ortho_of(mode, gram, other, narrow, wide, tall, square):
    size = gram.shape[0]
    vmem = pl.BlockSpec(memory_space=pltpu.VMEM)
    spec = [pl.BlockSpec(memory_space=pltpu.SMEM), vmem, vmem, vmem]
    spec += [pl.BlockSpec(memory_space=pl.ANY)] * (2 * CHIPS + 1)
    return plain_call(
        ortho_kernel,
        [like(wide[0].shape, bf16), like(tall.shape, bf16), like(square[0].shape, bf16)],
        [
            pltpu.VMEM((size, size), bf16),
            pltpu.VMEM(narrow.shape, bf16),
            pltpu.VMEM((size, wide[0].shape[1]), bf16),
            pltpu.VMEM(tall.shape, bf16),
            pltpu.VMEM((size, square[0].shape[1]), bf16),
            pltpu.SemaphoreType.DMA((CHIPS,)),
        ]
        + poly_scratch(1, size)
        + poly_scratch(1, narrow.shape[0]),
        in_specs=spec,
        cost_estimate=cost(100 * size * size * size, 8 * size * size),
    )(mode, gram, other, narrow, *wide, tall, *square)


def on_device(
    tokens_in,
    cotangent,
    block_order,
    weight_query,
    weight_key,
    weight_value,
    weight_out,
    weight_gate,
    weight_up,
    weight_down,
    moment_query,
    moment_key,
    moment_value,
    moment_out,
    moment_gate,
    moment_up,
    moment_down,
    small_params,
):
    repeat = lax.axis_size("r")
    cores = lax.axis_size("f")
    plane = CHIPS * cores
    ctx_count = repeat * LINE * CHIPS
    device_count = ctx_count * cores
    depth_count = repeat * LINE
    r_index = lax.axis_index("r")
    z_index = lax.axis_index("z")
    xy_index = lax.axis_index("xy")
    f_index = lax.axis_index("f")
    ctx_index = (r_index * LINE + z_index) * CHIPS + xy_index

    seq_count, seq_rows, width = tokens_in.shape
    seq_length = seq_rows * ctx_count
    block_rows = seq_rows // 2
    all_tokens = seq_count * cores * seq_length
    row_count = seq_count * seq_rows
    kv_width = weight_key.shape[1]
    head_count = width // HEAD_DIM
    kv_count = kv_width // HEAD_DIM
    group = head_count // kv_count
    part_rows = weight_query.shape[0]
    hidden_width = weight_gate.shape[1]
    down_rows = weight_down.shape[0]
    units = depth_count * down_rows
    small_rows = small_params.shape[0]
    both_width = 2 * (width + kv_width)

    front = jnp.concatenate([weight_query, weight_key, weight_value, weight_out], axis=1)
    small_line = jnp.pad(small_params, (0, both_width - small_rows))[None, :]
    front = jnp.concatenate([front, small_line], axis=0).astype(bf16)
    front_all = lax.all_gather(front, EVERY, axis=0, tiled=False)

    def by_unit(weight):
        return weight.astype(bf16).reshape(part_rows, depth_count, plane, down_rows)

    gate_up = jnp.stack([by_unit(weight_gate), by_unit(weight_up)], axis=0)
    gate_up = gate_up.transpose(3, 0, 1, 2, 4).reshape(plane, 2, part_rows, units)
    gate_up = exchange(gate_up, PLANE)
    front_all, gate_up = lax.optimization_barrier((front_all, gate_up))
    gate_up = gate_up.transpose(1, 0, 2, 3).reshape(2, plane * part_rows, units)
    unit_rows = gate_up
    gate_up = lax.all_gather(gate_up, ("r", "z"), axis=0, tiled=False)
    if repeat > 1:
        gate_up = gate_up.transpose(1, 0, 2, 3).reshape(1, 2, width, units)
    down_mat = lax.all_gather(weight_down.astype(bf16), ("r", "z"), axis=0, tiled=True)

    attn_mats = front_all[:, :part_rows, :].reshape(width, both_width)
    small_vals = front_all[:, part_rows, :small_rows].reshape(1, -1).astype(f32)

    stored = jnp.arange(block_rows, dtype=jnp.int32)
    places = jnp.arange(ctx_count, dtype=jnp.int32)
    xy_places = xy_index ^ (places // (LINE * repeat))
    z_places = z_index ^ (places // repeat % LINE)
    places = ((places % repeat) * LINE + z_places) * CHIPS + xy_places
    blocks = block_order.reshape(ctx_count, 2)[places].reshape(2 * ctx_count)
    key_pos = (blocks[:, None] * block_rows + stored[None, :]).reshape(seq_length, 1)
    own_blocks = lax.dynamic_slice_in_dim(block_order, 2 * ctx_index, 2)
    query_pos = (own_blocks[:, None] * block_rows + stored[None, :]).reshape(seq_rows)
    cosine, sine = rope_tables(query_pos)
    cosine = jnp.tile(cosine, (seq_count, 4))
    sine = jnp.tile(jnp.concatenate([-sine, sine], axis=1), (seq_count, 2))
    query_pos = jnp.tile(query_pos, group)[None, :]
    front_all, key_pos, query_pos, cosine, sine = lax.optimization_barrier(
        (front_all, key_pos, query_pos, cosine, sine)
    )

    inputs = tokens_in.reshape(row_count, width)
    grad_low = cotangent.reshape(row_count, width)
    grads_plane = lax.all_gather(after(grad_low, unit_rows), PLANE, axis=0, tiled=False)
    heads_shape = (seq_count, head_count, seq_rows, HEAD_DIM)
    pairs_shape = (seq_count, kv_count, seq_rows, 2 * HEAD_DIM)
    rows_shape = (row_count, width)
    queries, pairs, normed_one = plain_call(
        front_kernel,
        [like(heads_shape, bf16), like(pairs_shape, bf16), like(rows_shape, bf16)],
        cost_estimate=cost(6 * row_count * width * both_width, 8 * width * width),
    )(inputs, attn_mats, small_vals, cosine, sine)
    pairs_all = gather_ctx(pairs)
    mixed = attend(queries, pairs_all, key_pos, query_pos)
    attn_low, residual, normed_two = plain_call(
        middle_kernel,
        [like(rows_shape, bf16), like(rows_shape, f32), like(rows_shape, bf16)],
        cost_estimate=cost(6 * row_count * width * width, 8 * width * width),
    )(mixed, inputs, attn_mats, small_vals)
    normed_plane = gather_plane(normed_two)

    cores_here = [f_index ^ (number // CHIPS) for number in range(plane)]
    chips_here = [xy_index ^ (number % CHIPS) for number in range(plane)]
    order = jnp.stack([chip * cores + core for chip, core in zip(chips_here, cores_here)])
    part_y, part_dh, feed_grads = feed_forward(
        normed_plane, order, grads_plane, gate_up, down_mat
    )
    own_dh, *low_dh = fold(part_dh[0], swap(part_dh[1], "f", 1))
    arrived = [swap(piece, "xy", step) for step, piece in enumerate(low_dh, 1)]

    def by_line(part):
        part = part.reshape((repeat, LINE, -1) + part.shape[1:])
        return part.transpose(1, 0, 2, 3)

    line_gate = exchange(by_line(after(feed_grads[0], own_dh)), "z")
    arrived, line_gate = lax.optimization_barrier((arrived, line_gate))
    line_up = exchange(by_line(after(feed_grads[1], line_gate)), "z")
    grad_residual, grad_attn, grad_mixed, grad_gain_two = plain_call(
        turnback_kernel,
        [like(rows_shape, f32), like(rows_shape, bf16), like(heads_shape, bf16), like((1, width), f32)],
        cost_estimate=cost(6 * row_count * width * width, 8 * width * width),
    )(own_dh, *arrived, residual, grad_low, attn_mats, small_vals)
    grad_queries, part_pairs = attend_back(queries, grad_mixed, pairs_all, key_pos, query_pos)
    grad_queries, line_up = lax.optimization_barrier((grad_queries, line_up))
    line_down = exchange(by_line(after(feed_grads[2], line_up)), "z")

    here = jnp.stack([f_index, xy_index, z_index])
    vmem = pl.BlockSpec(memory_space=pltpu.VMEM)
    smem = pl.BlockSpec(memory_space=pltpu.SMEM)
    part_shape = (CHIPS, depth_count, part_rows, 2 * width)
    grad_query_lin, query_own, query_other = plain_call(
        query_kernel,
        [like(rows_shape, bf16), like(part_shape, bf16), like(part_shape, bf16)],
        in_specs=[smem] + [vmem] * 6,
        cost_estimate=cost(12 * row_count * width * width, 8 * width * width),
    )(here, normed_one, grad_queries, attn_low, grad_attn, cosine, sine)
    query_other = swap(query_other, "f", 1)

    part_gu = jnp.stack([total(line_gate), total(line_up)], axis=1)
    if repeat > 1:
        part_gu = lax.psum_scatter(part_gu, "r", scatter_dimension=0, tiled=True)
    part_gu = part_gu.astype(bf16).reshape(2, plane, part_rows, units).transpose(1, 0, 2, 3)
    sum_gate, sum_up, fresh_gate, fresh_up, wide_updates = wide_update(
        exchange(part_gu, PLANE), moment_gate, moment_up, down_rows
    )

    own_pairs, line_down = lax.optimization_barrier((reduce_ctx(part_pairs), line_down))
    part_shape = (CHIPS, depth_count, part_rows + 1, 2 * kv_width)
    input_grad, other_own, other_other = plain_call(
        back_kernel,
        [like(rows_shape, f32), like(part_shape, bf16), like(part_shape, bf16)],
        [
            pltpu.VMEM((row_count, width + 2 * kv_width), bf16),
            pltpu.VMEM((1, small_vals.shape[1]), f32),
        ],
        in_specs=[smem] + [vmem] * 10,
        cost_estimate=cost(6 * row_count * width * width, 8 * width * width),
    )(
        here,
        own_pairs,
        grad_query_lin,
        normed_one,
        inputs,
        grad_residual,
        attn_mats,
        small_vals,
        cosine,
        sine,
        grad_gain_two,
    )
    input_grad = input_grad.reshape(seq_count, seq_rows, width)
    own_sum, *low_sums = join(query_own, query_other, other_own, swap(other_other, "f", 1))
    low_sums = [swap(piece, "xy", step) for step, piece in enumerate(low_sums, 1)]
    own_sum, *low_sums = spread(own_sum, low_sums, repeat)
    low_sums = [swap(piece, "z", step) for step, piece in enumerate(low_sums, 1)]
    if repeat > 1:
        for piece in low_sums:
            own_sum += piece.astype(f32)
        own_sum = lax.psum_scatter(own_sum, "r", scatter_dimension=0, tiled=True)
        low_sums = [jnp.zeros(own_sum.shape, bf16)] * (LINE - 1)
    attn_sums, attn_fresh, small_line, mine, other = step_of(
        f_index.reshape(1),
        own_sum,
        low_sums,
        (moment_query, moment_key, moment_value, moment_out),
    )
    sum_small = small_line[0, :small_rows]

    sum_down = total(line_down)
    if repeat > 1:
        sum_down = lax.psum_scatter(sum_down, "r", scatter_dimension=0, tiled=True)
    sum_down = sum_down.reshape(down_rows, width)
    fresh_down = momentum_decay * moment_down + sum_down
    update_down = (sum_down + momentum_decay * fresh_down).astype(bf16)

    masters = (
        weight_query,
        weight_key,
        weight_value,
        weight_out,
        weight_gate,
        weight_up,
        weight_down,
    )
    new_moments = (*attn_fresh, fresh_gate, fresh_up, fresh_down)
    summed = (*attn_sums, sum_gate, sum_up, sum_down)

    half = hidden_width // cores
    all_rows = repeat * part_rows

    def whole_rows(piece, axis):
        if repeat > 1:
            piece = lax.all_gather(piece, "r", axis=axis, tiled=True)
        return piece

    def core_order(mine, other, axis):
        first = jnp.where(f_index == 0, mine, other)
        second = jnp.where(f_index == 0, other, mine)
        return jnp.concatenate([first, second], axis=axis)

    def to_line(piece, planes):
        def keep(source, target):
            return target in planes

        here = piece
        if len(planes) > 1:
            here = place(piece, jnp.minimum(z_index, 1))
        parts = [here]
        for step in range(1, LINE):
            chunk = piece
            if len(planes) > 1:
                chunk = place(piece, (z_index ^ step) % 2)
            parts.append(swap(chunk, "z", step, keep))
        return jnp.concatenate(parts, axis=0)

    def over_chips(rows, planes):
        return [rows] + [plane_swap(rows, step, planes) for step in range(1, CHIPS)]

    tall = over_chips(to_line(whole_rows(update_down, 0), (2,)), (2,))
    wide_updates = whole_rows(wide_updates, 1)
    wide_mine = lax.dynamic_slice_in_dim(wide_updates, f_index * half, half, 2)
    wide_other = lax.dynamic_slice_in_dim(wide_updates, (1 - f_index) * half, half, 2)
    wide_rows = core_order(wide_mine, swap(wide_other, "f", 1), 1)
    wide = over_chips(to_line(wide_rows, (0, 1)), (0, 1))
    mine = whole_rows(mine, 0)
    other = whole_rows(other, 0)
    both = core_order(mine, swap(other, "f", 1), 0)
    square = over_chips(to_line(both, (3,)), (3,))

    y_first, y_second = after(tuple(part_y), query_own)
    y_second = swap(y_second, "f", 1)
    own_y, *low_y = fold(*after((y_first, y_second), other_own))

    mode = jnp.maximum(z_index - 1, 0).reshape(1)
    mode, own_y, low_y = lax.optimization_barrier((mode, own_y, low_y))
    gram, narrow = gram_of(mode, wide, tall, square)
    low_y = after(low_y, gram)
    arrived_y = [swap(piece, "xy", step) for step, piece in enumerate(low_y, 1)]
    line_pairs = [(z * cores + i, z * cores + 1 - i) for z in range(LINE - 1) for i in range(cores)]
    gram_other = lax.ppermute(gram, ("z", "f"), line_pairs)
    wide_o, tall_o, square_o = ortho_of(
        mode, gram, gram_other, narrow, wide, tall[0], square
    )
    arrived_y = after(arrived_y, square_o)

    def from_line(piece, planes):
        parts = piece.reshape((LINE, -1) + piece.shape[1:])

        def keep(source, target):
            return source in planes

        arrived = [parts[0]] + [
            swap(parts[step], "z", step, keep) for step in range(1, LINE)
        ]
        chosen = []
        for number in planes:
            which = z_index ^ number
            value = arrived[0]
            for step in range(1, LINE):
                value = jnp.where(which == step, arrived[step], value)
            chosen.append(value)
        return chosen

    def own_of(piece, core, axis):
        start = core * all_rows + r_index * part_rows
        return lax.dynamic_slice_in_dim(piece, start, part_rows, axis)

    square_o = from_line(square_o, (3,))[0]
    wide_o = jnp.stack(from_line(wide_o, (0, 1)), axis=0)
    tall_o = from_line(tall_o, (2,))[0]
    if repeat > 1:
        tall_o = lax.dynamic_slice_in_dim(tall_o, r_index * down_rows, down_rows, 0)
    mine = own_of(square_o, f_index, 0)
    other = swap(own_of(square_o, 1 - f_index, 0), "f", 1)
    first = jnp.where(f_index == 0, mine, other)
    second = jnp.where(f_index == 0, other, mine)
    wide_mine = own_of(wide_o, f_index, 1)
    wide_other = swap(own_of(wide_o, 1 - f_index, 1), "f", 1)
    ortho_wide = core_order(wide_mine, wide_other, 2)

    activations = residual + own_y
    for piece in arrived_y:
        activations += piece.astype(f32)
    activations = activations.astype(bf16).reshape(seq_count, seq_rows, width)

    orthogonal = (
        first[:, :width],
        first[:, width:],
        second[:, width:],
        second[:, :width],
        ortho_wide[0],
        ortho_wide[1],
        tall_o,
    )
    new_masters = []
    for master, piece in zip(masters, orthogonal):
        factor = math.sqrt(max(1.0, master.shape[1] / (master.shape[0] * device_count)))
        new_masters.append(master - (muon_rate * factor) * piece.astype(f32))
    new_small = small_params - plain_rate / math.sqrt(all_tokens) * sum_small
    return (
        activations,
        input_grad,
        *summed,
        *new_masters,
        *new_moments,
        sum_small,
        new_small,
    )


def solution(mesh):
    cores = mesh.shape["fsdp"]
    chips = mesh.shape["ctx"] // (4 * LINE)
    fine = Mesh(mesh.devices.reshape(chips, LINE, 4, cores), EVERY)
    token_spec = P("f", CTX, None)
    shard_spec = P(EVERY, None)
    return jax.shard_map(
        on_device,
        mesh=fine,
        in_specs=(token_spec, token_spec, P()) + (shard_spec,) * 14 + (P(EVERY),),
        out_specs=(token_spec, token_spec) + (shard_spec,) * 21 + (P(EVERY), P(EVERY)),
        check_vma=False,
    )
```

```python
import functools
import math

import jax
import jax.numpy as jnp
from jax import lax
from jax.experimental import pallas as pl
from jax.experimental.pallas import tpu as pltpu
from jax.sharding import Mesh
from jax.sharding import PartitionSpec as P

HEAD_DIM = 64
NS_STEPS = 5
LINE = 4
VMEM_LIMIT = 56 * 1024 * 1024

theta_base = 1000000.0
norm_eps = 1e-06
ns_coeffs = (3.4445, -4.775, 2.0315)
momentum_decay = 0.95
muon_rate = 1.5
plain_rate = 2.0

EVERY = ("r", "z", "xy", "f")
CTX = ("r", "z", "xy")
PLANE = ("xy", "f")
CHIPS = 4

f32 = jnp.float32
bf16 = jnp.bfloat16


def rope_tables(positions):
    frequency = theta_base ** (-jnp.arange(0, HEAD_DIM, 2, dtype=f32) / HEAD_DIM)
    angles = positions.astype(f32)[:, None] * frequency[None, :]
    return (jnp.cos(angles), jnp.sin(angles))


def dot_nn(left_side, right_side):
    return jnp.dot(left_side, right_side, preferred_element_type=f32)


def dot_tn(left_side, right_side):
    return lax.dot_general(
        left_side, right_side, (((0,), (0,)), ((), ())), preferred_element_type=f32
    )


def dot_nt(left_side, right_side):
    return lax.dot_general(
        left_side, right_side, (((1,), (1,)), ((), ())), preferred_element_type=f32
    )


def after(value, event):
    return lax.optimization_barrier((value, event))


def exchange(parts, axes):
    return lax.all_to_all(parts, axes, split_axis=0, concat_axis=0, tiled=True)


def total(parts):
    return jnp.sum(parts.astype(f32), axis=0)


def swap(piece, axis, step, keep=None):
    count = lax.axis_size(axis)
    pairs = [(i, i ^ step) for i in range(count) if keep is None or keep(i, i ^ step)]
    return lax.ppermute(piece, axis, pairs)


def plane_swap(piece, step, depths):
    count = lax.axis_size("xy")
    pairs = [(z * count + i, z * count + (i ^ step)) for z in depths for i in range(count)]
    return lax.ppermute(piece, ("z", "xy"), pairs)


def gather_plane(piece):
    chips = [piece] + [swap(piece, "xy", step) for step in range(1, CHIPS)]
    return chips + [swap(each, "f", 1) for each in chips]


def place(parts, index):
    return lax.dynamic_index_in_dim(parts, index, 0, keepdims=False)


def gather_ctx(piece):
    if lax.axis_size("r") > 1:
        piece = lax.all_gather(piece, "r", axis=0, tiled=False)
    else:
        piece = piece[None]
    piece = jnp.concatenate([piece] + [swap(piece, "z", step) for step in range(1, LINE)], axis=0)
    return [piece] + [swap(piece, "xy", step) for step in range(1, CHIPS)]


def reduce_ctx(parts, event):
    repeat = lax.axis_size("r")
    chips = parts[0].astype(f32)
    for step in range(1, CHIPS):
        chips += swap(parts[step], "xy", step).astype(f32)
    chips, event = after(chips, event)
    chips = chips.reshape((LINE, repeat) + chips.shape[1:])
    low = chips.astype(bf16)
    own = chips[0]
    for step in range(1, LINE):
        own += swap(low[step], "z", step).astype(f32)
    if repeat > 1:
        own = lax.psum_scatter(own, "r", scatter_dimension=0, tiled=True)
    return own[0], event


def plain_call(kernel, out_shape, scratch=(), **keywords):
    return pl.pallas_call(
        kernel,
        out_shape=out_shape,
        scratch_shapes=list(scratch),
        compiler_params=pltpu.CompilerParams(vmem_limit_bytes=VMEM_LIMIT),
        **keywords,
    )


def cost(flops, moved):
    return pl.CostEstimate(flops=1, bytes_accessed=1, transcendentals=0)


def like(shape, dtype):
    return jax.ShapeDtypeStruct(shape, dtype)


def turn(values):
    lane = lax.broadcasted_iota(jnp.int32, values.shape, 1)
    low_half = lane % HEAD_DIM < HEAD_DIM // 2
    right = pltpu.roll(values, HEAD_DIM // 2, 1)
    left = pltpu.roll(values, 2 * HEAD_DIM - HEAD_DIM // 2, 1)
    return jnp.where(low_half, left, right)


def normed(values):
    rescale = lax.rsqrt(jnp.mean(values * values, axis=1, keepdims=True) + norm_eps)
    return values * rescale, rescale


def norm_back(grad_normed, plain, rescale, gain):
    inner = grad_normed * gain
    grad_in = rescale * (inner - plain * jnp.mean(inner * plain, axis=1, keepdims=True))
    return grad_in, jnp.sum(grad_normed * plain, axis=0, keepdims=True)


def front_kernel(x_ref, w_ref, small_ref, cos_ref, sin_ref, q_ref, pair_ref, h_ref):
    seqs, heads, rows, _ = q_ref.shape
    width = x_ref.shape[1]
    wide = w_ref.shape[1] - width
    plain, _ = normed(x_ref[...].astype(f32))
    low = (plain * small_ref[:, :width]).astype(bf16)
    h_ref[...] = low
    lin = dot_nn(low, w_ref[:, :wide]) + small_ref[:, 2 * width :]
    pair = 2 * HEAD_DIM
    cosine, sine = cos_ref[...], sin_ref[...]
    for j in range(heads // 2 + 1):
        both = lin[:, j * pair : (j + 1) * pair]
        both = (both * cosine + turn(both) * sine).astype(bf16)
        for b in range(seqs):
            span = slice(b * rows, (b + 1) * rows)
            for k in range(2):
                head = both[span, k * HEAD_DIM : (k + 1) * HEAD_DIM]
                if j < heads // 2:
                    q_ref[b, 2 * j + k] = head
                else:
                    start = wide - pair + k * HEAD_DIM
                    value = lin[span, start : start + HEAD_DIM].astype(bf16)
                    pair_ref[b, k] = jnp.concatenate([head, value], axis=1)


def middle_kernel(o_ref, x_ref, w_ref, small_ref, low_ref, x1_ref, h_ref):
    seqs, heads, rows, _ = o_ref.shape
    width = x_ref.shape[1]
    pair = 2 * HEAD_DIM
    for b in range(seqs):
        for j in range(heads // 2):
            both = jnp.concatenate([o_ref[b, 2 * j], o_ref[b, 2 * j + 1]], axis=1)
            low_ref[b * rows : (b + 1) * rows, j * pair : (j + 1) * pair] = both
    wide = w_ref.shape[1] - width
    residual = x_ref[...].astype(f32) + dot_nn(low_ref[...], w_ref[:, wide:])
    x1_ref[...] = residual
    plain, _ = normed(residual)
    h_ref[...] = (plain * small_ref[:, width : 2 * width]).astype(bf16)


def fold_kernel(a_ref, b_ref, own_ref, *low_refs):
    rows = own_ref.shape[0]
    own_ref[...] = a_ref[:rows].astype(f32) + b_ref[:rows].astype(f32)
    for step, ref in enumerate(low_refs, 1):
        span = slice(step * rows, (step + 1) * rows)
        ref[...] = (a_ref[span].astype(f32) + b_ref[span].astype(f32)).astype(bf16)


def fold(first, second):
    rows, width = first.shape
    rows //= CHIPS
    return plain_call(
        fold_kernel, [like((rows, width), f32)] + [like((rows, width), bf16)] * (CHIPS - 1)
    )(first, second)


def join_kernel(qa_ref, qb_ref, ka_ref, kb_ref, own_ref, *low_refs):
    wide = qa_ref.shape[3]
    for step, ref in enumerate((own_ref,) + low_refs):
        query = qa_ref[step].astype(f32) + qb_ref[step].astype(f32)
        other = ka_ref[step].astype(f32) + kb_ref[step].astype(f32)
        ref[:, :, :wide] = query.astype(ref.dtype)
        ref[:, :, wide:] = other.astype(ref.dtype)


def join(query_first, query_second, other_first, other_second):
    depth, rows, wide = query_first.shape[1:]
    shape = (depth, rows, wide + other_first.shape[3])
    return plain_call(join_kernel, [like(shape, f32)] + [like(shape, bf16)] * (CHIPS - 1))(
        query_first, query_second, other_first, other_second
    )


def spread_kernel(own_ref, a_ref, b_ref, c_ref, out_ref, *low_refs):
    repeat = out_ref.shape[0]
    for step, ref in enumerate((out_ref,) + low_refs):
        for r in range(repeat):
            q = r * LINE + step
            value = own_ref[q] + a_ref[q].astype(f32) + b_ref[q].astype(f32) + c_ref[q].astype(f32)
            ref[r] = value.astype(ref.dtype)


def spread(own, arrived, repeat):
    shape = (repeat,) + own.shape[1:]
    return plain_call(spread_kernel, [like(shape, f32)] + [like(shape, bf16)] * (LINE - 1))(
        own, *arrived
    )


def step_kernel(core_ref, own_ref, a_ref, b_ref, c_ref, *refs):
    moments, grads, fresh_refs = refs[:4], refs[4:8], refs[8:12]
    small_ref, mine_ref, other_ref = refs[12:]
    rows = moments[0].shape[0]
    total_sum = own_ref[0] + a_ref[0].astype(f32) + b_ref[0].astype(f32) + c_ref[0].astype(f32)
    width = moments[0].shape[1]
    narrow = moments[1].shape[1]
    starts = (0, 2 * width, 2 * width + narrow, width)
    small_ref[...] = total_sum[rows : rows + 1, 2 * width :]
    updates = []
    for m_ref, g_ref, n_ref, start in zip(moments, grads, fresh_refs, starts):
        grad = total_sum[:rows, start : start + m_ref.shape[1]]
        fresh = momentum_decay * m_ref[...] + grad
        g_ref[...] = grad
        n_ref[...] = fresh
        updates.append((grad + momentum_decay * fresh).astype(bf16))
    query, key, value, out = updates
    first = jnp.concatenate([query, key], axis=1)
    second = jnp.concatenate([out, value], axis=1)

    @pl.when(core_ref[0] == 0)
    def _():
        mine_ref[...] = first
        other_ref[...] = second

    @pl.when(core_ref[0] != 0)
    def _():
        mine_ref[...] = second
        other_ref[...] = first


def step_of(core, own, arrived, moments):
    rows = moments[0].shape[0]
    shapes = [like(m.shape, f32) for m in moments]
    pair_width = moments[0].shape[1] + moments[1].shape[1]
    vmem = pl.BlockSpec(memory_space=pltpu.VMEM)
    outs = plain_call(
        step_kernel,
        shapes
        + shapes
        + [like((1, 2 * moments[1].shape[1]), f32)]
        + [like((rows, pair_width), bf16)] * 2,
        in_specs=[pl.BlockSpec(memory_space=pltpu.SMEM)] + [vmem] * 8,
    )(core, own, *arrived, *moments)
    return outs[:4], outs[4:8], outs[8], outs[9], outs[10]


def turnback_kernel(
    own_ref, a_ref, b_ref, c_ref, x1_ref, dy_ref, w_ref, small_ref, dx_ref, da_ref, do_ref, gain_ref
):
    seqs, heads, rows, _ = do_ref.shape
    width = x1_ref.shape[1]
    wide = w_ref.shape[1] - width
    grad = own_ref[...] + a_ref[...].astype(f32) + b_ref[...].astype(f32) + c_ref[...].astype(f32)
    plain, rescale = normed(x1_ref[...])
    grad_in, grad_gain = norm_back(grad, plain, rescale, small_ref[:, width : 2 * width])
    gain_ref[...] = grad_gain
    grad_residual = dy_ref[...].astype(f32) + grad_in
    dx_ref[...] = grad_residual
    low = grad_residual.astype(bf16)
    da_ref[...] = low
    mixed = dot_nt(low, w_ref[:, wide:]).astype(bf16)
    for b in range(seqs):
        for j in range(heads):
            start = j * HEAD_DIM
            do_ref[b, j] = mixed[b * rows : (b + 1) * rows, start : start + HEAD_DIM]


def shard_rows(here_ref, refs, pieces_of, first, column):
    chips, depth = refs[0].shape[:2]
    core, chip, line = here_ref[0], here_ref[1], here_ref[2]
    for k in range(2):
        for target, ref in enumerate(refs):

            @pl.when((core ^ k) == target)
            def _():
                for q in range(depth):
                    for c in range(chips):
                        piece = pieces_of((q * chips + c) * 2 + k)
                        at = (q // LINE) * LINE + ((q % LINE) ^ line)
                        rows = slice(first, first + piece.shape[0])
                        ref[c ^ chip, at, rows, column : column + piece.shape[1]] = piece


def rows_of(value, rows):
    return lambda number: value[number * rows : (number + 1) * rows]


def query_kernel(
    here_ref, h_ref, dq_ref, o_ref, da_ref, cos_ref, sin_ref, lin_ref, own_ref, other_ref
):
    seqs, heads, rows, _ = dq_ref.shape
    width = h_ref.shape[1]
    pair = 2 * HEAD_DIM
    for b in range(seqs):
        span = slice(b * rows, (b + 1) * rows)
        cosine, sine = cos_ref[span], sin_ref[span]
        for j in range(heads // 2):
            both = jnp.concatenate([dq_ref[b, 2 * j], dq_ref[b, 2 * j + 1]], axis=1)
            both = both * cosine - turn(both) * sine
            lin_ref[span, j * pair : (j + 1) * pair] = both.astype(bf16)
    for ref in (own_ref, other_ref):
        ref[...] = jnp.zeros_like(ref)
    rows = width // (2 * own_ref.shape[0] * own_ref.shape[1])
    query = dot_tn(h_ref[...], lin_ref[...]).astype(bf16)
    shard_rows(here_ref, (own_ref, other_ref), rows_of(query, rows), 0, 0)
    out = dot_tn(o_ref[...], da_ref[...]).astype(bf16)
    shard_rows(here_ref, (own_ref, other_ref), rows_of(out, rows), 0, width)


def back_kernel(
    here_ref,
    pair_ref,
    lin_ref,
    h_ref,
    x_ref,
    dx_ref,
    w_ref,
    small_ref,
    cos_ref,
    sin_ref,
    gain_ref,
    out_ref,
    own_ref,
    other_ref,
    all_lin,
    all_small,
):
    seqs, kv_heads, rows, pair = pair_ref.shape
    width = x_ref.shape[1]
    wide = w_ref.shape[1] - width
    all_lin[:, :width] = lin_ref[...]
    for b in range(seqs):
        span = slice(b * rows, (b + 1) * rows)
        first, second = pair_ref[b, 0], pair_ref[b, 1]
        keys = jnp.concatenate([first[:, :HEAD_DIM], second[:, :HEAD_DIM]], axis=1)
        values = jnp.concatenate([first[:, HEAD_DIM:], second[:, HEAD_DIM:]], axis=1)
        keys = keys * cos_ref[span] - turn(keys) * sin_ref[span]
        all_lin[span, width : width + pair] = keys.astype(bf16)
        all_lin[span, width + pair :] = values.astype(bf16)
    lin = all_lin[...]
    grad = dot_nt(lin, w_ref[:, :wide])
    plain, rescale = normed(x_ref[...].astype(f32))
    grad_in, grad_gain = norm_back(grad, plain, rescale, small_ref[:, :width])
    out_ref[...] = dx_ref[...] + grad_in
    all_small[:, :width] = grad_gain
    all_small[:, width : 2 * width] = gain_ref[...]
    all_small[:, 2 * width :] = jnp.sum(lin.astype(f32), axis=0, keepdims=True)
    refs = (own_ref, other_ref)
    count = 2 * own_ref.shape[0] * own_ref.shape[1]
    for ref in refs:
        ref[...] = jnp.zeros_like(ref)
    grads = dot_tn(h_ref[...], lin[:, width:]).astype(bf16)
    shard_rows(here_ref, refs, rows_of(grads, width // count), 0, 0)
    small_rows = all_small.shape[1] // count

    def small_of(number):
        return all_small[:, number * small_rows : (number + 1) * small_rows].astype(bf16)

    shard_rows(here_ref, refs, small_of, width // count, 0)


def softmax_keys(keys, queries, key_pos, query_pos):
    scores = dot_nt(keys, queries) * (HEAD_DIM ** (-0.5))
    masked = jnp.where(key_pos <= query_pos, scores, -1e30)
    terms = jnp.exp(masked - jnp.max(masked, axis=0, keepdims=True))
    return terms * (1.0 / jnp.sum(terms, axis=0, keepdims=True))


def joined_pairs(refs):
    return jnp.concatenate([ref[...].reshape(-1, ref.shape[-1]) for ref in refs], axis=0)


def attend_kernel(q_ref, *refs):
    kv_refs, (kpos_ref, qpos_ref, o_ref) = refs[:CHIPS], refs[CHIPS:]
    group, rows, width = q_ref.shape[1:]
    queries = q_ref[...].reshape(group * rows, width)
    pairs = joined_pairs(kv_refs)
    probs = softmax_keys(pairs[:, :width], queries, kpos_ref[...], qpos_ref[...]).astype(bf16)
    mixed = dot_nn(pairs.T[width:], probs)
    o_ref[...] = mixed.T.reshape(1, group, rows, width).astype(bf16)


def attend_back_kernel(q_ref, do_ref, *refs):
    kv_refs, (kpos_ref, qpos_ref, dq_ref), dkv_refs = (
        refs[:CHIPS],
        refs[CHIPS : CHIPS + 3],
        refs[CHIPS + 3 :],
    )
    group, rows, width = q_ref.shape[1:]
    queries = q_ref[...].reshape(group * rows, width)
    grads = do_ref[...].reshape(group * rows, width)
    pairs = joined_pairs(kv_refs)
    probs = softmax_keys(pairs[:, :width], queries, kpos_ref[...], qpos_ref[...])
    grad_probs = dot_nt(pairs[:, width:], grads)
    delta = jnp.sum(probs * grad_probs, axis=0, keepdims=True)
    grad_scores = (probs * (grad_probs - delta)).astype(bf16)
    scale = HEAD_DIM ** (-0.5)
    grad_keys = dot_nn(grad_scores, queries) * scale
    grad_values = dot_nn(probs.astype(bf16), grads)
    both = jnp.concatenate([grad_keys, grad_values], axis=1).astype(bf16)
    span = both.shape[0] // CHIPS
    for number, ref in enumerate(dkv_refs):
        ref[...] = both[number * span : (number + 1) * span].reshape(ref.shape)
    grad_queries = dot_nn(pairs.T[:width], grad_scores) * scale
    dq_ref[...] = grad_queries.T.reshape(dq_ref.shape)


def attention_specs(queries, pairs):
    _, heads, rows, _ = queries.shape
    chunks, _, kv_heads = pairs.shape[:3]
    group = heads // kv_heads
    length = CHIPS * chunks * rows
    q_spec = pl.BlockSpec((1, group, rows, HEAD_DIM), lambda b, h: (b, h, 0, 0))
    kv_spec = pl.BlockSpec((chunks, 1, 1, rows, 2 * HEAD_DIM), lambda b, h: (0, b, h, 0, 0))
    kpos_spec = pl.BlockSpec((length, 1), lambda b, h: (0, 0))
    qpos_spec = pl.BlockSpec((1, group * rows), lambda b, h: (0, 0))
    return q_spec, kv_spec, kpos_spec, qpos_spec


def attend(queries, pairs, key_pos, query_pos):
    q_spec, kv_spec, kpos_spec, qpos_spec = attention_specs(queries, pairs[0])
    scores = queries.shape[0] * queries.shape[1] * queries.shape[2] * key_pos.shape[0]
    return plain_call(
        attend_kernel,
        like(queries.shape, bf16),
        grid=(queries.shape[0], pairs[0].shape[2]),
        in_specs=[q_spec] + [kv_spec] * CHIPS + [kpos_spec, qpos_spec],
        out_specs=q_spec,
        cost_estimate=cost(scores * 16 * HEAD_DIM, scores * 8),
    )(queries, *pairs, key_pos, query_pos)


def attend_back(queries, grads, pairs, key_pos, query_pos):
    q_spec, kv_spec, kpos_spec, qpos_spec = attention_specs(queries, pairs[0])
    scores = queries.shape[0] * queries.shape[1] * queries.shape[2] * key_pos.shape[0]
    outs = plain_call(
        attend_back_kernel,
        [like(queries.shape, f32)] + [like(pairs[0].shape, bf16)] * CHIPS,
        grid=(queries.shape[0], pairs[0].shape[2]),
        in_specs=[q_spec, q_spec] + [kv_spec] * CHIPS + [kpos_spec, qpos_spec],
        out_specs=[q_spec] + [kv_spec] * CHIPS,
        cost_estimate=cost(scores * 40 * HEAD_DIM, scores * 12),
    )(queries, grads, *pairs, key_pos, query_pos)
    return outs[0], outs[1:]


def feed_kernel(count, *refs):
    h_refs, dy_refs = refs[:count], refs[count : 2 * count]
    wgu_ref, wd_ref = refs[2 * count : 2 * count + 2]
    y_refs = refs[2 * count + 2 : 2 * count + 4]
    dh_refs = refs[2 * count + 4 : 2 * count + 6]
    ggu_ref, gd_ref, agu, ad, h_all, dy_all, sems = refs[2 * count + 6 :]
    step = pl.program_id(0)
    rows = h_refs[0].shape[0]
    tile = y_refs[0].shape[0]
    each = tile // rows

    def copies(number):
        span = pl.ds(number * rows, rows)
        return (
            pltpu.make_async_copy(h_refs[number], h_all.at[span], sems.at[0, number]),
            pltpu.make_async_copy(dy_refs[number], dy_all.at[span], sems.at[1, number]),
        )

    @pl.when(step == 0)
    def _():
        for number in range(count):
            for copy in copies(number):
                copy.start()
        agu[...] = jnp.zeros_like(agu)
        ad[...] = jnp.zeros_like(ad)

    for number in range(count):

        @pl.when(step == number // each)
        def _():
            for copy in copies(number):
                copy.wait()

    start = pl.multiple_of(step * tile, tile)
    normed_rows = h_all[pl.ds(start, tile)]
    grads = dy_all[pl.ds(start, tile)]
    units = wgu_ref.shape[3]
    gate_mat = wgu_ref[:, 0].reshape(-1, units)
    up_mat = wgu_ref[:, 1].reshape(-1, units)
    gate = dot_nn(normed_rows, gate_mat)
    up = dot_nn(normed_rows, up_mat)
    sigmoid = 1.0 / (1.0 + jnp.exp(-gate))
    silu = gate * sigmoid
    hidden = (silu * up).astype(bf16)
    grad_hidden = dot_nt(grads, wd_ref[...])
    grad_gate = (grad_hidden * up * sigmoid * (1.0 + gate * (1.0 - sigmoid))).astype(bf16)
    grad_up = (grad_hidden * silu).astype(bf16)
    dh = (dot_nt(grad_gate, gate_mat) + dot_nt(grad_up, up_mat)).astype(bf16)
    y = dot_nn(hidden, wd_ref[...]).astype(bf16)
    for core in range(2):

        @pl.when(step // (pl.num_programs(0) // 2) == core)
        def _():
            y_refs[core][...] = y
            dh_refs[core][...] = dh

    agu[0] += dot_tn(normed_rows, grad_gate)
    agu[1] += dot_tn(normed_rows, grad_up)
    ad[...] += dot_tn(hidden, grads)

    @pl.when(step == pl.num_programs(0) - 1)
    def _():
        repeat, height = ggu_ref.shape[2:4]
        depth = gd_ref.shape[2]
        for r in range(repeat):
            for z in range(LINE):
                start = (r * LINE + z) * height
                for which in range(2):
                    ggu_ref[z, which, r] = agu[which, start : start + height].astype(bf16)
                start = (r * LINE + z) * depth
                gd_ref[z, r] = ad[start : start + depth].astype(bf16)


def feed_forward(normed_rows, grads, gate_up, down_mat, repeat):
    count = len(normed_rows)
    rows, width = normed_rows[0].shape
    units = gate_up.shape[3]
    tokens = count * rows
    tile = CHIPS * rows
    steps = count // CHIPS
    half = tokens // 2
    first = pl.BlockSpec((tile, width), lambda t: (jnp.minimum(t, steps // 2 - 1), 0))
    second = pl.BlockSpec((tile, width), lambda t: (jnp.maximum(t - steps // 2, 0), 0))
    weights = pl.BlockSpec(gate_up.shape, lambda t: (0, 0, 0, 0))
    wide_shape = (LINE, 2, repeat, width // (LINE * repeat), units)
    tall_shape = (LINE, repeat, units // (LINE * repeat), width)
    wide = pl.BlockSpec(wide_shape, lambda t: (0, 0, 0, 0, 0))
    tall_out = pl.BlockSpec(tall_shape, lambda t: (0, 0, 0, 0))
    tall = pl.BlockSpec((units, width), lambda t: (0, 0))
    anywhere = pl.BlockSpec(memory_space=pl.ANY)
    outs = plain_call(
        functools.partial(feed_kernel, count),
        [like((half, width), bf16)] * 4
        + [like(wide_shape, bf16), like(tall_shape, bf16)],
        [
            pltpu.VMEM((2, width, units), f32),
            pltpu.VMEM((units, width), f32),
            pltpu.VMEM((tokens, width), bf16),
            pltpu.VMEM((tokens, width), bf16),
            pltpu.SemaphoreType.DMA((2, count)),
        ],
        grid=(steps,),
        in_specs=[anywhere] * (2 * count) + [weights, tall],
        out_specs=[first, second, first, second, wide, tall_out],
        cost_estimate=cost(36 * tokens * width * units, 8 * tokens * width + 12 * units * width),
    )(*normed_rows, *grads, gate_up, down_mat)
    return outs[:2], outs[2:4], outs[4], outs[5]


def update_kernel(span, in_ref, mg_ref, mu_ref, gg_ref, gu_ref, ng_ref, nu_ref, u_ref):
    plane, _, _, units = in_ref.shape
    depth = units // span
    triples = ((mg_ref, gg_ref, ng_ref), (mu_ref, gu_ref, nu_ref))
    for which, (m_ref, g_ref, n_ref) in enumerate(triples):
        for q in range(depth):
            for p in range(plane):
                start = (q * plane + p) * span
                piece = in_ref[p, which, :, q * span : (q + 1) * span]
                g_ref[:, start : start + span] = piece.astype(f32)
        grad = g_ref[...]
        fresh = momentum_decay * m_ref[...] + grad
        n_ref[...] = fresh
        u_ref[which] = (grad + momentum_decay * fresh).astype(bf16)


def wide_update(arrived, moment_gate, moment_up, span):
    rows, columns = moment_gate.shape
    return plain_call(
        functools.partial(update_kernel, span),
        [like((rows, columns), f32)] * 4 + [like((2, rows, columns), bf16)],
    )(arrived, moment_gate, moment_up)


def row_spans(size):
    first = size % 256
    bounds = ([0, first] if first else [0]) + list(range(first + 256, size + 1, 256))
    return list(zip(bounds[:-1], bounds[1:]))


def poly_scratch(count, size):
    return [pltpu.VMEM((count, size, size), bf16)] * 6 + [pltpu.VMEM((2, count, size, size), bf16)] * 2


def poly_core(count, size, load, write, scratch):
    a_hi, a_lo, p_hi, p_lo, t_hi, t_lo, q_hi, q_lo = scratch
    alpha_term, beta_term, gamma_term = ns_coeffs
    spans = row_spans(size)

    def eye_of(start, stop):
        row = lax.broadcasted_iota(jnp.int32, (stop - start, size - start), 0)
        col = lax.broadcasted_iota(jnp.int32, (stop - start, size - start), 1)
        return row == col

    def store(high, low, i, start, stop, value):
        rounded = value.astype(bf16)
        rest = (value - rounded.astype(f32)).astype(bf16)
        high[i, start:stop, start:] = rounded
        low[i, start:stop, start:] = rest
        if stop < size:
            turned = value[:, stop - start :].T
            rounded = turned.astype(bf16)
            high[i, stop:, start:stop] = rounded
            low[i, stop:, start:stop] = (turned - rounded.astype(f32)).astype(bf16)

    def product(left, right, i, start, stop):
        left_hi, left_lo = left[0][i, start:stop, :], left[1][i, start:stop, :]
        right_hi, right_lo = right[0][i, :, start:], right[1][i, :, start:]
        return (
            dot_nn(left_hi, right_lo) + dot_nn(left_lo, right_hi) + dot_nn(left_hi, right_hi)
        )

    grams = (a_hi, a_lo)
    poly = (p_hi, p_lo)
    once = (t_hi, t_lo)
    inverses = []
    for i in range(count):
        squares = jnp.zeros((1, 1), f32)
        for start, stop in spans:
            diagonal = jnp.where(eye_of(start, stop), load(i, start, stop), 0.0)
            squares += jnp.sum(jnp.sum(diagonal, axis=1, keepdims=True), axis=0, keepdims=True)
        inverse = 1.0 / (jnp.sqrt(squares) + 1e-07)
        inverses.append(inverse)
        for start, stop in spans:
            store(*grams, i, start, stop, load(i, start, stop) * (inverse * inverse))

    for sweep in range(NS_STEPS):
        now, later = sweep % 2, (sweep + 1) % 2
        old = (q_hi.at[later], q_lo.at[later])
        new = (q_hi.at[now], q_lo.at[now])
        for start, stop in spans:
            for i in range(count):
                value = gamma_term * product(grams, grams, i, start, stop)
                mine = a_hi[i, start:stop, start:].astype(f32)
                mine += a_lo[i, start:stop, start:].astype(f32)
                value += beta_term * mine
                value += jnp.where(eye_of(start, stop), alpha_term, 0.0)
                store(*poly, i, start, stop, value)
                if sweep == 0:
                    store(*new, i, start, stop, value * inverses[i])
        last = sweep == NS_STEPS - 1
        if sweep > 0:
            for start, stop in spans:
                for i in range(count):
                    value = product(old, poly, i, start, stop)
                    if not last:
                        store(*new, i, start, stop, value)
                    else:
                        write(i, slice(start, stop), slice(start, size), value)
                        if stop < size:
                            turned = value[:, stop - start :].T
                            write(i, slice(stop, size), slice(start, stop), turned)
        if not last:
            for left, target in ((grams, once), (once, grams)):
                for start, stop in spans:
                    for i in range(count):
                        store(*target, i, start, stop, product(left, poly, i, start, stop))


def load_blocks(refs, target, sem):
    rows = refs[0].shape[0]
    return [
        pltpu.make_async_copy(ref, target.at[pl.ds(number * rows, rows)], sem.at[number])
        for number, ref in enumerate(refs)
    ]


def upper_gram(out_ref, whole, contract_rows, size):
    for start, stop in row_spans(size):
        if contract_rows:
            block = dot_tn(whole[:, start:stop], whole[:, start:size])
        else:
            block = dot_nt(whole[start:stop, :], whole[start:, :])
        out_ref[start:stop, start:] = block


def gram_kernel(mode_ref, *refs):
    groups = (refs[:CHIPS], refs[CHIPS : 2 * CHIPS])
    out_ref, *scratch, sem = refs[2 * CHIPS :]
    for number, (group, whole) in enumerate(zip(groups, scratch)):

        @pl.when(mode_ref[0] == number)
        def _():
            copies = load_blocks(group, whole, sem)
            for copy in copies:
                copy.start()
            for copy in copies:
                copy.wait()
            upper_gram(out_ref, whole, number == 1, out_ref.shape[0])


def gram_of(mode, wide, tall):
    size = tall[0].shape[1]
    spec = [pl.BlockSpec(memory_space=pltpu.SMEM)]
    spec += [pl.BlockSpec(memory_space=pl.ANY)] * (2 * CHIPS)
    scratch = [
        pltpu.VMEM((CHIPS * group[0].shape[0], group[0].shape[1]), bf16) for group in (wide, tall)
    ]
    return plain_call(
        gram_kernel,
        like((size, size), f32),
        scratch + [pltpu.SemaphoreType.DMA((CHIPS,))],
        in_specs=spec,
        cost_estimate=cost(4 * size * size * size * 3, 8 * size * size),
    )(mode, *wide, *tall)


def square_gram_kernel(mode_ref, *refs):
    group = refs[:CHIPS]
    out_ref, narrow_ref, whole, sem = refs[CHIPS:]
    size = out_ref.shape[0]

    @pl.when(mode_ref[0] == 2)
    def _():
        copies = load_blocks(group, whole, sem)
        for copy in copies:
            copy.start()
        for copy in copies:
            copy.wait()
        upper_gram(out_ref, whole.at[:, :size], False, size)
        narrow = whole[:, size:]
        narrow_ref[...] = dot_tn(narrow, narrow)


def square_gram_of(mode, square, size):
    narrow = square[0].shape[1] - size
    spec = [pl.BlockSpec(memory_space=pltpu.SMEM)]
    spec += [pl.BlockSpec(memory_space=pl.ANY)] * CHIPS
    return plain_call(
        square_gram_kernel,
        [like((size, size), f32), like((narrow, narrow), f32)],
        [
            pltpu.VMEM((CHIPS * square[0].shape[0], square[0].shape[1]), bf16),
            pltpu.SemaphoreType.DMA((CHIPS,)),
        ],
        in_specs=spec,
        cost_estimate=cost(4 * size * size * size * 3, 8 * size * size),
    )(mode, *square)


def stack_kernel(*refs):
    out_ref = refs[-1]
    rows = refs[0].shape[0]
    for number, ref in enumerate(refs[:-1]):
        out_ref[number * rows : (number + 1) * rows] = ref[...]


def stack_rows(pieces):
    rows, width = pieces[0].shape
    return plain_call(stack_kernel, like((len(pieces) * rows, width), bf16))(*pieces)


def ortho_kernel(mode_ref, a_ref, b_ref, c_ref, n_ref, *refs):
    wide, tall, square = refs[:CHIPS], refs[CHIPS : CHIPS + 1], refs[CHIPS + 1 : 2 * CHIPS + 1]
    outs = refs[2 * CHIPS + 1 : 2 * CHIPS + 4]
    q_ref, k_ref, *wholes, sem = refs[2 * CHIPS + 4 : 2 * CHIPS + 10]
    scratch = refs[2 * CHIPS + 10 : 2 * CHIPS + 18]
    narrow_scratch = refs[2 * CHIPS + 18 :]
    groups = (wide, tall, square)
    for number, (group, whole) in enumerate(zip(groups, wholes)):

        @pl.when(mode_ref[0] == number)
        def _():
            for copy in load_blocks(group, whole, sem):
                copy.start()

    def load(i, start, stop):
        pair = a_ref[start:stop, start:] + b_ref[start:stop, start:]
        return jnp.where(mode_ref[0] == 2, c_ref[start:stop, start:], pair)

    def write(i, rows, columns, value):
        q_ref[rows, columns] = value.astype(bf16)

    size = a_ref.shape[0]
    poly_core(1, size, load, write, scratch)

    @pl.when(mode_ref[0] == 2)
    def _():
        def narrow_load(i, start, stop):
            return n_ref[start:stop, start:]

        def narrow_write(i, rows, columns, value):
            k_ref[rows, columns] = value.astype(bf16)

        poly_core(1, n_ref.shape[0], narrow_load, narrow_write, narrow_scratch)

    for number, (group, whole, out_ref) in enumerate(zip(groups, wholes, outs)):

        @pl.when(mode_ref[0] == number)
        def _():
            for copy in load_blocks(group, whole, sem):
                copy.wait()
            if number == 1:
                out_ref[...] = dot_nn(whole[...], q_ref[...]).astype(bf16)
            elif number == 0:
                rows = q_ref[: out_ref.shape[0], :]
                out_ref[...] = dot_nn(rows, whole[...]).astype(bf16)
            else:
                count = out_ref.shape[0]
                rows = q_ref[:count, :]
                out_ref[:, :size] = dot_nn(rows, whole[:, :size]).astype(bf16)
                out_ref[:, size:] = dot_nn(whole[:count, size:], k_ref[...]).astype(bf16)


def ortho_of(mode, gram, other, third, narrow, wide, tall, square):
    size = gram.shape[0]
    vmem = pl.BlockSpec(memory_space=pltpu.VMEM)
    spec = [pl.BlockSpec(memory_space=pltpu.SMEM), vmem, vmem, vmem, vmem]
    spec += [pl.BlockSpec(memory_space=pl.ANY)] * (2 * CHIPS + 1)
    return plain_call(
        ortho_kernel,
        [like(wide[0].shape, bf16), like(tall.shape, bf16), like(square[0].shape, bf16)],
        [
            pltpu.VMEM((size, size), bf16),
            pltpu.VMEM(narrow.shape, bf16),
            pltpu.VMEM((size, wide[0].shape[1]), bf16),
            pltpu.VMEM(tall.shape, bf16),
            pltpu.VMEM((size, square[0].shape[1]), bf16),
            pltpu.SemaphoreType.DMA((CHIPS,)),
        ]
        + poly_scratch(1, size)
        + poly_scratch(1, narrow.shape[0]),
        in_specs=spec,
        cost_estimate=cost(100 * size * size * size, 8 * size * size),
    )(mode, gram, other, third, narrow, *wide, tall, *square)


def on_device(
    tokens_in,
    cotangent,
    block_order,
    weight_query,
    weight_key,
    weight_value,
    weight_out,
    weight_gate,
    weight_up,
    weight_down,
    moment_query,
    moment_key,
    moment_value,
    moment_out,
    moment_gate,
    moment_up,
    moment_down,
    small_params,
):
    repeat = lax.axis_size("r")
    cores = lax.axis_size("f")
    plane = CHIPS * cores
    ctx_count = repeat * LINE * CHIPS
    device_count = ctx_count * cores
    depth_count = repeat * LINE
    r_index = lax.axis_index("r")
    z_index = lax.axis_index("z")
    xy_index = lax.axis_index("xy")
    f_index = lax.axis_index("f")
    ctx_index = (r_index * LINE + z_index) * CHIPS + xy_index

    seq_count, seq_rows, width = tokens_in.shape
    seq_length = seq_rows * ctx_count
    block_rows = seq_rows // 2
    all_tokens = seq_count * cores * seq_length
    row_count = seq_count * seq_rows
    kv_width = weight_key.shape[1]
    head_count = width // HEAD_DIM
    kv_count = kv_width // HEAD_DIM
    group = head_count // kv_count
    part_rows = weight_query.shape[0]
    hidden_width = weight_gate.shape[1]
    down_rows = weight_down.shape[0]
    units = depth_count * down_rows
    small_rows = small_params.shape[0]
    both_width = 2 * (width + kv_width)

    front = jnp.concatenate([weight_query, weight_key, weight_value, weight_out], axis=1)
    small_line = jnp.pad(small_params, (0, both_width - small_rows))[None, :]
    front = jnp.concatenate([front, small_line], axis=0).astype(bf16)
    front_all = lax.all_gather(front, EVERY, axis=0, tiled=False)

    def by_unit(weight):
        return weight.astype(bf16).reshape(part_rows, depth_count, plane, down_rows)

    gate_up = jnp.stack([by_unit(weight_gate), by_unit(weight_up)], axis=0)
    gate_up = gate_up.transpose(3, 0, 1, 2, 4).reshape(plane, 2, part_rows, units)
    gate_up = exchange(gate_up, PLANE)
    grad_low = cotangent.reshape(row_count, width)
    grads_plane = gather_plane(grad_low)
    front_all, gate_up, grads_plane = lax.optimization_barrier((front_all, gate_up, grads_plane))
    gate_up = gate_up.transpose(1, 0, 2, 3).reshape(2, plane * part_rows, units)
    gate_up = lax.all_gather(gate_up, ("r", "z"), axis=0, tiled=False)
    if repeat > 1:
        gate_up = gate_up.transpose(1, 0, 2, 3).reshape(1, 2, width, units)
    down_mat = lax.all_gather(weight_down.astype(bf16), ("r", "z"), axis=0, tiled=True)

    attn_mats = front_all[:, :part_rows, :].reshape(width, both_width)
    small_vals = front_all[:, part_rows, :small_rows].reshape(1, -1).astype(f32)

    stored = jnp.arange(block_rows, dtype=jnp.int32)
    places = jnp.arange(ctx_count, dtype=jnp.int32)
    xy_places = xy_index ^ (places // (LINE * repeat))
    z_places = z_index ^ (places // repeat % LINE)
    places = ((places % repeat) * LINE + z_places) * CHIPS + xy_places
    blocks = block_order.reshape(ctx_count, 2)[places].reshape(2 * ctx_count)
    key_pos = (blocks[:, None] * block_rows + stored[None, :]).reshape(seq_length, 1)
    own_blocks = lax.dynamic_slice_in_dim(block_order, 2 * ctx_index, 2)
    query_pos = (own_blocks[:, None] * block_rows + stored[None, :]).reshape(seq_rows)
    cosine, sine = rope_tables(query_pos)
    cosine = jnp.tile(cosine, (seq_count, 4))
    sine = jnp.tile(jnp.concatenate([-sine, sine], axis=1), (seq_count, 2))
    query_pos = jnp.tile(query_pos, group)[None, :]
    front_all, key_pos, query_pos, cosine, sine = lax.optimization_barrier(
        (front_all, key_pos, query_pos, cosine, sine)
    )

    inputs = tokens_in.reshape(row_count, width)
    heads_shape = (seq_count, head_count, seq_rows, HEAD_DIM)
    pairs_shape = (seq_count, kv_count, seq_rows, 2 * HEAD_DIM)
    rows_shape = (row_count, width)
    queries, pairs, normed_one = plain_call(
        front_kernel,
        [like(heads_shape, bf16), like(pairs_shape, bf16), like(rows_shape, bf16)],
        cost_estimate=cost(6 * row_count * width * both_width, 8 * width * width),
    )(inputs, attn_mats, small_vals, cosine, sine)
    pairs_all = gather_ctx(pairs)
    mixed = attend(queries, pairs_all, key_pos, query_pos)
    attn_low, residual, normed_two = plain_call(
        middle_kernel,
        [like(rows_shape, bf16), like(rows_shape, f32), like(rows_shape, bf16)],
        cost_estimate=cost(6 * row_count * width * width, 8 * width * width),
    )(mixed, inputs, attn_mats, small_vals)
    normed_plane = gather_plane(normed_two)

    here = jnp.stack([f_index, xy_index, z_index])
    part_y, part_dh, line_gu, part_down = feed_forward(
        normed_plane, grads_plane, gate_up, down_mat, repeat
    )
    own_dh, *low_dh = fold(part_dh[0], swap(part_dh[1], "f", 1))
    arrived = [swap(piece, "xy", step) for step, piece in enumerate(low_dh, 1)]
    line_gu, own_dh = after(line_gu, own_dh)
    line_gu = exchange(line_gu, "z")
    grad_residual, grad_attn, grad_mixed, grad_gain_two = plain_call(
        turnback_kernel,
        [like(rows_shape, f32), like(rows_shape, bf16), like(heads_shape, bf16), like((1, width), f32)],
        cost_estimate=cost(6 * row_count * width * width, 8 * width * width),
    )(own_dh, *arrived, residual, grad_low, attn_mats, small_vals)
    grad_queries, part_pairs = attend_back(queries, grad_mixed, pairs_all, key_pos, query_pos)
    grad_queries, line_gu = lax.optimization_barrier((grad_queries, line_gu))

    vmem = pl.BlockSpec(memory_space=pltpu.VMEM)
    smem = pl.BlockSpec(memory_space=pltpu.SMEM)
    padded = -(-(part_rows + 1) // 8) * 8
    part_shape = (CHIPS, depth_count, padded, 2 * width)
    grad_query_lin, query_own, query_other = plain_call(
        query_kernel,
        [like(rows_shape, bf16), like(part_shape, bf16), like(part_shape, bf16)],
        in_specs=[smem] + [vmem] * 6,
        cost_estimate=cost(12 * row_count * width * width, 8 * width * width),
    )(here, normed_one, grad_queries, attn_low, grad_attn, cosine, sine)
    query_other = swap(query_other, "f", 1)

    part_gu = total(line_gu)
    if repeat > 1:
        part_gu = lax.psum_scatter(part_gu, "r", scatter_dimension=1, tiled=True)
    part_gu = part_gu.astype(bf16).reshape(2, plane, part_rows, units).transpose(1, 0, 2, 3)
    part_gu, part_pairs = after(part_gu, part_pairs)
    part_gu = exchange(part_gu, PLANE)
    part_gu, part_down = after(part_gu, part_down)
    line_down = exchange(part_down, "z")
    sum_gate, sum_up, fresh_gate, fresh_up, wide_updates = wide_update(
        part_gu, moment_gate, moment_up, down_rows
    )

    own_pairs, grad_query_lin = reduce_ctx(part_pairs, grad_query_lin)
    own_pairs, wide_updates = lax.optimization_barrier((own_pairs, wide_updates))
    part_shape = (CHIPS, depth_count, padded, 2 * kv_width)
    input_grad, other_own, other_other = plain_call(
        back_kernel,
        [like(rows_shape, f32), like(part_shape, bf16), like(part_shape, bf16)],
        [
            pltpu.VMEM((row_count, width + 2 * kv_width), bf16),
            pltpu.VMEM((1, small_vals.shape[1]), f32),
        ],
        in_specs=[smem] + [vmem] * 10,
        cost_estimate=cost(6 * row_count * width * width, 8 * width * width),
    )(
        here,
        own_pairs,
        grad_query_lin,
        normed_one,
        inputs,
        grad_residual,
        attn_mats,
        small_vals,
        cosine,
        sine,
        grad_gain_two,
    )
    input_grad = input_grad.reshape(seq_count, seq_rows, width)
    sum_down = total(line_down)
    if repeat > 1:
        sum_down = lax.psum_scatter(sum_down, "r", scatter_dimension=0, tiled=True)
    sum_down = sum_down.reshape(down_rows, width)
    fresh_down = momentum_decay * moment_down + sum_down
    update_down = (sum_down + momentum_decay * fresh_down).astype(bf16)

    half = hidden_width // cores
    all_rows = repeat * part_rows

    def whole_rows(piece, axis):
        if repeat > 1:
            piece = lax.all_gather(piece, "r", axis=axis, tiled=True)
        return piece

    def core_order(mine, other, axis):
        first = jnp.where(f_index == 0, mine, other)
        second = jnp.where(f_index == 0, other, mine)
        return jnp.concatenate([first, second], axis=axis)

    def to_line(piece, planes, put=functools.partial(jnp.concatenate, axis=0)):
        def keep(source, target):
            return target in planes

        here = piece
        if len(planes) > 1:
            here = place(piece, jnp.minimum(z_index, 1))
        parts = [here]
        for step in range(1, LINE):
            chunk = piece
            if len(planes) > 1:
                chunk = place(piece, (z_index ^ step) % 2)
            parts.append(swap(chunk, "z", step, keep))
        return put(parts)

    def over_chips(rows, planes):
        return [rows] + [plane_swap(rows, step, planes) for step in range(1, CHIPS)]

    tall_line = to_line(whole_rows(update_down, 0), (2,))
    wide_updates = whole_rows(wide_updates, 1)
    wide_mine = lax.dynamic_slice_in_dim(wide_updates, f_index * half, half, 2)
    wide_other = lax.dynamic_slice_in_dim(wide_updates, (1 - f_index) * half, half, 2)
    wide_rows = core_order(wide_mine, swap(wide_other, "f", 1), 1)
    wide_line = to_line(wide_rows, (0, 1))

    part_y, query_own = after(part_y, query_own)
    y_second = swap(part_y[1], "f", 1)
    (y_first, y_second), other_own = after((part_y[0], y_second), other_own)
    own_y, *low_y = fold(y_first, y_second)

    other_other = swap(other_other, "f", 1)
    own_sum, *low_sums = join(query_own, query_other, other_own, other_other)
    own_sum, wide_line, tall_line = lax.optimization_barrier((own_sum, wide_line, tall_line))
    wide = over_chips(wide_line, (0, 1))
    tall = over_chips(tall_line, (2,))
    low_sums = [swap(piece, "xy", step) for step, piece in enumerate(low_sums, 1)]
    masters = (
        weight_query,
        weight_key,
        weight_value,
        weight_out,
        weight_gate,
        weight_up,
        weight_down,
    )
    low_sums, wide, tall = lax.optimization_barrier((low_sums, wide, tall))
    mode = jnp.maximum(z_index - 1, 0).reshape(1)
    gram = gram_of(mode, wide, tall)
    line_pairs = [(z * cores + i, z * cores + 1 - i) for z in range(LINE - 1) for i in range(cores)]
    gram_other = lax.ppermute(gram, ("z", "f"), line_pairs)
    own_sum, *low_sums = spread(own_sum, low_sums, repeat)
    low_sums = [swap(piece, "z", step) for step, piece in enumerate(low_sums, 1)]
    if repeat > 1:
        for piece in low_sums:
            own_sum += piece.astype(f32)
        own_sum = lax.psum_scatter(own_sum, "r", scatter_dimension=0, tiled=True)
        low_sums = [jnp.zeros(own_sum.shape, bf16)] * (LINE - 1)
    own_sum, low_y, gram = lax.optimization_barrier((own_sum, low_y, gram))
    attn_sums, attn_fresh, small_line, mine, other = step_of(
        f_index.reshape(1),
        own_sum,
        low_sums,
        (moment_query, moment_key, moment_value, moment_out),
    )
    sum_small = small_line[0, :small_rows]
    new_moments = (*attn_fresh, fresh_gate, fresh_up, fresh_down)
    summed = (*attn_sums, sum_gate, sum_up, sum_down)
    mine = whole_rows(mine, 0)
    other = whole_rows(other, 0)
    both = core_order(mine, swap(other, "f", 1), 0)
    square = over_chips(to_line(both, (3,), stack_rows), (3,))
    line_rows = LINE * cores * all_rows

    square_gram, narrow = square_gram_of(mode, square, width)
    low_y, square_gram = after(low_y, square_gram)
    arrived_y = [swap(piece, "xy", step) for step, piece in enumerate(low_y, 1)]
    wide_o, tall_o, square_o = ortho_of(
        mode, gram, gram_other, square_gram, narrow, wide, tall[0], square
    )
    arrived_y, square_o = after(arrived_y, square_o)

    def from_line(piece, planes):
        parts = piece.reshape((LINE, -1) + piece.shape[1:])

        def keep(source, target):
            return source in planes

        arrived = [parts[0]] + [
            swap(parts[step], "z", step, keep) for step in range(1, LINE)
        ]
        chosen = []
        for number in planes:
            which = z_index ^ number
            value = arrived[0]
            for step in range(1, LINE):
                value = jnp.where(which == step, arrived[step], value)
            chosen.append(value)
        return chosen

    def own_of(piece, core, axis):
        start = core * all_rows + r_index * part_rows
        return lax.dynamic_slice_in_dim(piece, start, part_rows, axis)

    square_o = from_line(square_o, (3,))[0]
    wide_o = jnp.stack(from_line(wide_o, (0, 1)), axis=0)
    tall_o = from_line(tall_o, (2,))[0]
    if repeat > 1:
        tall_o = lax.dynamic_slice_in_dim(tall_o, r_index * down_rows, down_rows, 0)
    mine = own_of(square_o, f_index, 0)
    other = swap(own_of(square_o, 1 - f_index, 0), "f", 1)
    first = jnp.where(f_index == 0, mine, other)
    second = jnp.where(f_index == 0, other, mine)
    wide_mine = own_of(wide_o, f_index, 1)
    wide_other = swap(own_of(wide_o, 1 - f_index, 1), "f", 1)
    ortho_wide = core_order(wide_mine, wide_other, 2)

    activations = residual + own_y
    for piece in arrived_y:
        activations += piece.astype(f32)
    activations = activations.astype(bf16).reshape(seq_count, seq_rows, width)

    orthogonal = (
        first[:, :width],
        first[:, width:],
        second[:, width:],
        second[:, :width],
        ortho_wide[0],
        ortho_wide[1],
        tall_o,
    )
    new_masters = []
    for master, piece in zip(masters, orthogonal):
        factor = math.sqrt(max(1.0, master.shape[1] / (master.shape[0] * device_count)))
        new_masters.append(master - (muon_rate * factor) * piece.astype(f32))
    new_small = small_params - plain_rate / math.sqrt(all_tokens) * sum_small
    return (
        activations,
        input_grad,
        *summed,
        *new_masters,
        *new_moments,
        sum_small,
        new_small,
    )


def solution(mesh):
    cores = mesh.shape["fsdp"]
    chips = mesh.shape["ctx"] // (4 * LINE)
    fine = Mesh(mesh.devices.reshape(chips, LINE, 4, cores), EVERY)
    token_spec = P("f", CTX, None)
    shard_spec = P(EVERY, None)
    return jax.shard_map(
        on_device,
        mesh=fine,
        in_specs=(token_spec, token_spec, P()) + (shard_spec,) * 14 + (P(EVERY),),
        out_specs=(token_spec, token_spec) + (shard_spec,) * 21 + (P(EVERY), P(EVERY)),
        check_vma=False,
    )
```
